128 devices in a mesh: dp: 32 (over x, y, z_lo), mp: 4 (over z_hi, core).
Axes of the slice: x: 4, y: 4, z: 4 (z_hi: 2, z_lo: 2; z = z_hi * 2 + z_lo), core: 2. Of those that a mesh axis runs over, the one named last changes fastest.
Arguments:
- hidden: bfloat16 [6144, 5120], P('dp'), may hold values from -14 to 14
- w_query: bfloat16 [5120, 4096], P('dp', 'mp'), may hold values from -0.15625 to 0.15625
- w_key: bfloat16 [5120, 512], P('dp', 'mp'), may hold values from -0.078125 to 0.078125
- w_value: bfloat16 [5120, 512], P('dp', 'mp'), may hold values from -0.078125 to 0.078125
- out_grad: bfloat16 [6144, 4096], P('dp', 'mp'), may hold values from -6 to 6
- lengths: int32 [4], replicated, may hold values from 1 to 5376, 6144 in all
- advantages: float32 [4], replicated, may hold values from -4 to 4
Outputs:
- attended: bfloat16 [6144, 4096], P('dp', 'mp')
- grad_hidden: bfloat16 [6144, 5120], P('dp', 'mp')
- grad_w_query: bfloat16 [5120, 4096], P('dp', 'mp')
- grad_w_key: bfloat16 [5120, 512], P('dp', 'mp')
- grad_w_value: bfloat16 [5120, 512], P('dp', 'mp')
The draws below stay inside these ranges and needn't reach their ends.
Inputs may be any that keep to these rules, and one draw needn't show every extreme that they name: Response r occupies the next lengths[r] tokens of the stream, in order; the lengths sum to 6144.
All inputs are finite; a program needn't handle non-finite values.
Results may differ from the reference program's by a relative error of at most 0.039.
Values may be sent and summed in bfloat16 or wider, within the bound.
No kernel may reach another device: no remote copies, remote signals or barrier semaphores. Data moves between devices by JAX's collectives and lax.ppermute only.
A program may use at most 128 MiB of HBM per device.

```python
import math
import jax
import jax.numpy as jnp
import numpy as np
from jax import lax

D = 5120
HEADS = 32
KV_HEADS = 4
HEAD_DIM = 128
TOK_DEV = 192
NRESP = 4
TOKENS = 6144
LONGEST = 5376
N_DP = 32
N_MP = 4


def draw_hidden(key, part):
    key = jax.random.fold_in(key, 11)
    base_key = jax.random.fold_in(key, 0)
    base = jax.random.normal(base_key, (TOKENS, D), jnp.float32)
    return jnp.clip(base, -6.0, 6.0).astype(jnp.bfloat16)


def block_levels(own_key, dims, shards, low, top_value):
    gain = 1.0
    for dim, parts in shards:
        draws = jax.random.uniform(jax.random.fold_in(jax.random.fold_in(own_key, 6), dim), (parts,), jnp.float32, low / len(shards), top_value / len(shards))
        gain = gain * jnp.repeat(jnp.exp(draws), dims[dim] // parts).reshape((-1,) + (1,) * (len(dims) - 1 - dim))
    return gain


def profile(number_of, total, limit, skew):
    loads = [(1 << 20) // math.isqrt(standing ** skew) + 1 for standing in range(2, number_of + 1)]
    surplus, counts = total - limit - (number_of - 1), [1] * (number_of - 1)
    while surplus > 0:
        candidates = [i for i in range(number_of - 1) if counts[i] < limit]
        whole, remaining = sum([loads[i] for i in candidates]), surplus
        for i in candidates:
            addition = min(limit - counts[i], max(1, remaining * loads[i] // whole), surplus)
            counts[i] = counts[i] + addition
            surplus = surplus - addition
    return np.array([limit] + counts)


def ragged_sizes(key, amount, total, reach, skew):
    if amount == 2:
        one = jax.random.randint(key, (), max(1, total - reach), min(reach, total - 1) + 1)
        return jnp.stack([one, total - one])
    sizes = jnp.asarray(profile(amount, total, reach, skew), jnp.int32)
    couples = (amount - 1) // 2
    source_of, receiver = sizes[1:1 + 2 * couples:2], sizes[2:2 + 2 * couples:2]
    margin = jnp.minimum(source_of - 1, reach - receiver)
    passed = jax.random.randint(jax.random.fold_in(key, 1), (couples,), 0, 1 << 20) % (margin + 1)
    sizes = sizes.at[1:1 + 2 * couples:2].set(source_of - passed).at[2:2 + 2 * couples:2].set(receiver + passed)
    return sizes[jax.random.permutation(jax.random.fold_in(key, 2), amount)]


def gaussian(key, dims, width, reach, pieces=(), kind=jnp.bfloat16):
    gain = block_levels(key, dims, pieces, -0.22, 0.18) if pieces else 1.0
    array = jax.random.normal(key, dims, jnp.float32) * width * gain
    return jnp.minimum(jnp.maximum(array, -reach), reach).astype(kind)


def setup_inputs(seed: int = 0) -> dict:
    seeds = jax.random.split(jax.random.key(seed), 8)
    return {
        "hidden": draw_hidden(jax.random.fold_in(seeds[7], 71), 0),
        "w_query": gaussian(seeds[1], (D, HEADS * HEAD_DIM), (D // 4) ** -0.5, 0.15625, ((0, 32), (1, 4))),
        "w_key": gaussian(seeds[2], (D, KV_HEADS * HEAD_DIM), D ** -0.5, 0.078125, ((0, 32), (1, 4))),
        "w_value": gaussian(seeds[3], (D, KV_HEADS * HEAD_DIM), D ** -0.5, 0.078125, ((0, 32), (1, 4))),
        "out_grad": gaussian(seeds[4], (TOKENS, HEADS * HEAD_DIM), 1.0, 6.0, ((0, 32), (1, 4))),
        "lengths": ragged_sizes(seeds[5], NRESP, TOKENS, LONGEST, 2).astype(jnp.int32),
        "advantages": gaussian(seeds[6], (NRESP,), 1.0, 4.0, (), jnp.float32),
    }


rope_theta = 1000000.0
neg_large = -1e+30

def locate(global_rows, lengths):
    boundary = jnp.cumsum(lengths)
    segment_ids = lax.optimization_barrier(jnp.sum((global_rows[:, None] >= boundary[None, :]).astype(jnp.int32), axis=1))
    starting = boundary - lengths
    member = segment_ids[:, None] == jnp.arange(lengths.shape[0], dtype=jnp.int32)[None, :]
    positions = global_rows - lax.optimization_barrier(jnp.sum(jnp.where(member, starting[None, :], 0), axis=1))
    return (segment_ids, positions, member)

def rotary_tables(positions, head_dim):
    half_dim = head_dim // 2
    exponent = jnp.arange(half_dim, dtype=jnp.float32) * (2.0 / head_dim)
    inverse = jnp.exp(-math.log(rope_theta) * exponent)
    angles = positions.astype(jnp.float32)[:, None] * inverse[None, :]
    return (jnp.cos(angles), jnp.sin(angles))

def rotate(values, cosine_table, sine_table, direction):
    half_dim = values.shape[-1] // 2
    first_half = values[..., :half_dim]
    second_half = values[..., half_dim:]
    cosine_part = cosine_table[:, None, :]
    sine_part = sine_table[:, None, :] * direction
    return jnp.concatenate([first_half * cosine_part - second_half * sine_part, second_half * cosine_part + first_half * sine_part], axis=-1)

def reference(hidden, w_query, w_key, w_value, out_grad, lengths, advantages):
    all_rows = jnp.arange(TOKENS, dtype=jnp.int32)
    segment_ids, positions, member = locate(all_rows, lengths)
    cosine_table, sine_table = rotary_tables(positions, HEAD_DIM)
    group_size = HEADS // KV_HEADS
    score_scale = 1.0 / math.sqrt(HEAD_DIM)
    queries = rotate(jnp.dot(hidden, w_query, preferred_element_type=jnp.float32).reshape(TOKENS, HEADS, HEAD_DIM), cosine_table, sine_table, 1.0).astype(jnp.bfloat16)
    keys = rotate(jnp.dot(hidden, w_key, preferred_element_type=jnp.float32).reshape(TOKENS, KV_HEADS, HEAD_DIM), cosine_table, sine_table, 1.0).astype(jnp.bfloat16)
    values = jnp.dot(hidden, w_value, preferred_element_type=jnp.float32).astype(jnp.bfloat16).reshape(TOKENS, KV_HEADS, HEAD_DIM)
    token_adv = lax.optimization_barrier(jnp.sum(jnp.where(member, advantages[None, :], 0.0), axis=1))
    token_grad = (out_grad.astype(jnp.float32) * token_adv[:, None]).astype(jnp.bfloat16)
    query_major = queries.reshape(TOKENS, KV_HEADS, group_size, HEAD_DIM).transpose(1, 0, 2, 3)
    grad_major = token_grad.reshape(TOKENS, KV_HEADS, group_size, HEAD_DIM).transpose(1, 0, 2, 3)
    key_major = keys.transpose(1, 0, 2)
    value_major = values.transpose(1, 0, 2)
    block_size = min(512, TOKENS)
    block_count = TOKENS // block_size

    def one_head(operands):
        query_head, key_head, value_head, grad_head = operands
        key_wide = key_head.astype(jnp.float32)
        value_wide = value_head.astype(jnp.float32)

        def one_block(running, block_index):
            key_acc, value_acc = running
            first_row = block_index * block_size
            query_block = lax.dynamic_slice_in_dim(query_head, first_row, block_size, 0).astype(jnp.float32)
            grad_block = lax.dynamic_slice_in_dim(grad_head, first_row, block_size, 0).astype(jnp.float32)
            block_rows = first_row + jnp.arange(block_size, dtype=jnp.int32)
            block_segments = lax.dynamic_slice_in_dim(segment_ids, first_row, block_size, 0)
            allowed = (all_rows[None, :] <= block_rows[:, None]) & (segment_ids[None, :] == block_segments[:, None])
            scores = jnp.einsum('tgd,ud->gtu', query_block, key_wide) * score_scale
            scores = jnp.where(allowed[None], scores, neg_large)
            top_score = lax.optimization_barrier(jnp.max(scores, axis=-1))
            log_total = top_score + jnp.log(lax.optimization_barrier(jnp.sum(jnp.where(allowed[None], jnp.exp(scores - top_score[..., None]), 0.0), axis=-1)))
            probs = jnp.where(allowed[None], jnp.exp(scores - log_total[..., None]), 0.0)
            rounded = lax.optimization_barrier(probs.astype(jnp.bfloat16)).astype(jnp.float32)
            attended_block = jnp.einsum('gtu,ud->tgd', rounded, value_wide).astype(jnp.bfloat16)
            row_delta = jnp.einsum('tgd,tgd->gt', attended_block.astype(jnp.float32), grad_block)
            prob_grad = jnp.einsum('tgd,ud->gtu', grad_block, value_wide)
            score_grad = lax.optimization_barrier((probs * (prob_grad - row_delta[..., None])).astype(jnp.bfloat16)).astype(jnp.float32)
            query_grad_block = jnp.einsum('gtu,ud->tgd', score_grad, key_wide) * score_scale
            key_acc = key_acc + jnp.einsum('gtu,tgd->ud', score_grad, query_block)
            value_acc = value_acc + jnp.einsum('gtu,tgd->ud', rounded, grad_block)
            return ((key_acc, value_acc), (attended_block, query_grad_block))
        empty = jnp.zeros((TOKENS, HEAD_DIM), jnp.float32)
        (key_acc, value_acc), (attended_blocks, query_blocks) = lax.scan(one_block, (empty, empty), jnp.arange(block_count, dtype=jnp.int32))
        return (attended_blocks.reshape(TOKENS, group_size, HEAD_DIM), query_blocks.reshape(TOKENS, group_size, HEAD_DIM), key_acc * score_scale, value_acc)
    attended_heads, query_heads, key_heads, value_heads = lax.map(one_head, (query_major, key_major, value_major, grad_major))
    attended = attended_heads.transpose(1, 0, 2, 3).reshape(TOKENS, HEADS * HEAD_DIM)
    query_rot = query_heads.transpose(1, 0, 2, 3).reshape(TOKENS, HEADS, HEAD_DIM)
    query_grad = rotate(query_rot, cosine_table, sine_table, -1.0).astype(jnp.bfloat16).reshape(TOKENS, HEADS * HEAD_DIM)
    key_grad = rotate(key_heads.transpose(1, 0, 2), cosine_table, sine_table, -1.0).astype(jnp.bfloat16).reshape(TOKENS, KV_HEADS * HEAD_DIM)
    value_grad = value_heads.transpose(1, 0, 2).astype(jnp.bfloat16).reshape(TOKENS, KV_HEADS * HEAD_DIM)
    grad_cat = jnp.concatenate([query_grad, key_grad, value_grad], axis=1)

    def add_block(running, block_index):
        hidden_block = lax.dynamic_slice_in_dim(hidden, block_index * TOK_DEV, TOK_DEV, 0)
        grad_block = lax.dynamic_slice_in_dim(grad_cat, block_index * TOK_DEV, TOK_DEV, 0)
        term = jnp.dot(hidden_block.T, grad_block, preferred_element_type=jnp.float32)
        return (running + lax.optimization_barrier(term.astype(jnp.bfloat16)).astype(jnp.float32), None)
    weight_total, _ = lax.scan(add_block, jnp.zeros((D, grad_cat.shape[1]), jnp.float32), jnp.arange(N_DP, dtype=jnp.int32))
    weight_total = weight_total.astype(jnp.bfloat16)
    query_cols = HEADS * HEAD_DIM
    key_cols = KV_HEADS * HEAD_DIM
    grad_w_query = weight_total[:, :query_cols]
    grad_w_key = weight_total[:, query_cols:query_cols + key_cols]
    grad_w_value = weight_total[:, query_cols + key_cols:]
    group_query = query_cols // N_MP
    group_key = key_cols // N_MP
    hidden_total = jnp.zeros((TOKENS, D), jnp.float32)
    for mp_group in range(N_MP):
        query_slice = slice(mp_group * group_query, (mp_group + 1) * group_query)
        key_slice = slice(mp_group * group_key, (mp_group + 1) * group_key)
        term = jnp.dot(query_grad[:, query_slice], w_query[:, query_slice].T, preferred_element_type=jnp.float32)
        term = term + jnp.dot(key_grad[:, key_slice], w_key[:, key_slice].T, preferred_element_type=jnp.float32)
        term = term + jnp.dot(value_grad[:, key_slice], w_value[:, key_slice].T, preferred_element_type=jnp.float32)
        hidden_total = hidden_total + lax.optimization_barrier(term.astype(jnp.bfloat16)).astype(jnp.float32)
    grad_hidden = hidden_total.astype(jnp.bfloat16)
    return (attended, grad_hidden, grad_w_query, grad_w_key, grad_w_value)
```

```python
import math

import jax
import jax.numpy as jnp
from jax import lax
from jax.experimental import pallas as pl
from jax.experimental.pallas import tpu as pltpu
from jax.sharding import Mesh, PartitionSpec as P

HEAD_DIM = 128
HALF = 64
ROPE_THETA = 1000000.0
NEG_LARGE = -1e30
SCALE = 1.0 / math.sqrt(HEAD_DIM)
LOG2E = 1.4426950408889634
SIDE = 4
PLANE = SIDE * SIDE
BLOCK = 384
VMEM_LIMIT = 56 * 1024 * 1024


def fetch(value, axis, step):
    return lax.ppermute(value, axis, [(i, (i - step) % SIDE) for i in range(SIDE)])


def push(value, axis, step):
    return lax.ppermute(value, axis, [(i, (i + step) % SIDE) for i in range(SIDE)])


def plane_index(x, y, c):
    return (x * SIDE + y) * 2 + c


def cross_push(value, step, first):
    pairs = []
    for x in range(SIDE):
        for y in range(SIDE):
            for c in range(2):
                along_x = (c == 0) == first
                target = ((x + step) % SIDE, y) if along_x else (x, (y + step) % SIDE)
                pairs.append((plane_index(x, y, c), plane_index(*target, c)))
    return lax.ppermute(value, ("x", "y", "c"), pairs)


def swap_core(value):
    return lax.ppermute(value, "c", [(0, 1), (1, 0)])


ROUND = [(0, 1), (3, 2), (1, 3), (2, 0)]
ROUND_BACK = [(b, a) for a, b in ROUND]
CROSS = [(1, 2), (2, 1)]


def regroup(half0, half1, zl, c):
    first = jnp.where(zl == 0, half0, half1)
    second = jnp.where(zl == 0, half1, half0)
    moved = lax.ppermute(second, ("zl", "c"), ROUND)
    crossed = lax.ppermute(first, ("zl", "c"), CROSS)
    own = jnp.where(zl == c, first, moved)
    other = jnp.where(zl == c, moved, crossed)
    return own, other


def ungroup(own, other, zl, c):
    moved = lax.ppermute(jnp.where(zl == c, other, own), ("zl", "c"), ROUND_BACK)
    crossed = lax.ppermute(other, ("zl", "c"), CROSS)
    first = jnp.where(zl == c, own, crossed)
    half0 = jnp.where(zl == 0, first, moved)
    half1 = jnp.where(zl == 0, moved, first)
    return half0, half1


def in_order(own, other, zl):
    return jnp.where(zl == 0, own, other), jnp.where(zl == 0, other, own)


def gather_rows(rows0, rows1):
    strips = []
    for rows, near, far in ((rows0, "x", "y"), (rows1, "y", "x")):
        line = jnp.concatenate([rows] + [fetch(rows, near, s) for s in (1, 2, 3)], axis=0)
        strips += [line] + [fetch(line, far, s) for s in (1, 2, 3)]
    return jnp.concatenate(strips, axis=0)


def total(parts):
    result = parts[0].astype(jnp.float32)
    for part in parts[1:]:
        result = result + part.astype(jnp.float32)
    return result.astype(jnp.bfloat16)


def scatter_rows(terms):
    half = terms.shape[0] // 2
    results = []
    for start, near, far in ((0, "x", "y"), (half, "y", "x")):
        chunk = half // SIDE
        strips = [terms[start + s * chunk : start + (s + 1) * chunk] for s in range(SIDE)]
        line = total([strips[0]] + [push(strips[s], far, s) for s in (1, 2, 3)])
        small = chunk // SIDE
        pieces = [line[s * small : (s + 1) * small] for s in range(SIDE)]
        results.append(total([pieces[0]] + [push(pieces[s], near, s) for s in (1, 2, 3)]))
    return results


def permute_body(index_ref, source_ref, result_ref):
    @pl.loop(0, result_ref.shape[0])
    def _(i):
        result_ref[i] = source_ref[index_ref[i]]


def permute_blocks(source, index):
    vmem = pl.BlockSpec(memory_space=pltpu.VMEM)
    return pl.pallas_call(
        permute_body,
        out_shape=jax.ShapeDtypeStruct(source.shape, source.dtype),
        in_specs=[pl.BlockSpec(memory_space=pltpu.SMEM), vmem],
        out_specs=vmem,
        compiler_params=pltpu.CompilerParams(vmem_limit_bytes=VMEM_LIMIT),
        cost_estimate=pl.CostEstimate(
            flops=0, bytes_accessed=2 * source.size * source.dtype.itemsize, transcendentals=0
        ),
    )(index, source)


def attention_body(
    scalar_ref,
    key_slot_ref,
    value_slot_ref,
    token_ref,
    lowest_ref,
    query_t_ref,
    query_ref,
    grad_t_ref,
    grad_ref,
    key_ref,
    value_ref,
    attended_ref,
    dquery_ref,
    dkey_ref,
    dvalue_ref,
    probs_ref,
    tops_ref,
):
    first_block = scalar_ref[0]
    last_block = scalar_ref[1]
    mask_below = scalar_ref[2]
    rows = query_t_ref.shape[1]
    token = token_ref[...]
    lowest = lowest_ref[...]

    dkey_ref[...] = jnp.zeros_like(dkey_ref)
    dvalue_ref[...] = jnp.zeros_like(dvalue_ref)

    def forward(b, carry):
        top, weight, output = carry
        keys = key_ref[key_slot_ref[b]]
        scores = jnp.dot(keys, query_t_ref[...], preferred_element_type=jnp.float32)
        scores = scores * (SCALE * LOG2E)

        def masked(s):
            position = b * BLOCK + lax.broadcasted_iota(jnp.int32, s.shape, 0)
            return jnp.where((position <= token) & (position >= lowest), s, NEG_LARGE)

        scores = lax.cond((b == last_block) | (b <= mask_below), masked, lambda s: s, scores)
        new_top = jnp.maximum(top, jnp.max(scores, axis=0, keepdims=True))
        probs = jnp.exp2(scores - new_top)
        fade = jnp.exp2(top - new_top)
        rounded = probs.astype(jnp.bfloat16)
        probs_ref[b] = rounded
        tops_ref[b] = new_top
        weight = weight * fade + jnp.sum(probs, axis=0, keepdims=True)
        values_t = value_ref[value_slot_ref[b]].T
        output = output * fade + jnp.dot(values_t, rounded, preferred_element_type=jnp.float32)
        return new_top, weight, output

    top, weight, output = lax.fori_loop(
        first_block,
        last_block + 1,
        forward,
        (
            jnp.full((1, rows), NEG_LARGE, jnp.float32),
            jnp.zeros((1, rows), jnp.float32),
            jnp.zeros((HEAD_DIM, rows), jnp.float32),
        ),
    )
    inverse = 1.0 / weight
    attended = (output * inverse).astype(jnp.bfloat16)
    attended_ref[...] = attended
    delta = jnp.sum(
        attended.astype(jnp.float32) * grad_t_ref[...].astype(jnp.float32), axis=0, keepdims=True
    )

    def backward(b, dquery):
        key_slot = key_slot_ref[b]
        value_slot = value_slot_ref[b]
        prob_grad = jnp.dot(value_ref[value_slot], grad_t_ref[...], preferred_element_type=jnp.float32)
        probs = probs_ref[b].astype(jnp.float32) * (jnp.exp2(tops_ref[b] - top) * inverse)
        score_grad = (probs * (prob_grad - delta)).astype(jnp.bfloat16)
        dvalue_ref[value_slot] = jnp.dot(
            probs.astype(jnp.bfloat16), grad_ref[...], preferred_element_type=jnp.float32
        )
        dkey_ref[key_slot] = jnp.dot(score_grad, query_ref[...], preferred_element_type=jnp.float32)
        return dquery + jnp.dot(key_ref[key_slot].T, score_grad, preferred_element_type=jnp.float32)

    dquery = lax.fori_loop(
        first_block, last_block + 1, backward, jnp.zeros((HEAD_DIM, rows), jnp.float32)
    )
    dquery_ref[...] = dquery * SCALE


def attention(scalars, key_slots, value_slots, token, lowest, query_t, grad_t, keys, values):
    rows = query_t.shape[1]
    vmem = pl.BlockSpec(memory_space=pltpu.VMEM)
    smem = pl.BlockSpec(memory_space=pltpu.SMEM)
    kv = jax.ShapeDtypeStruct((PLANE, BLOCK, HEAD_DIM), jnp.float32)
    pairs = PLANE * BLOCK * rows // 2
    return pl.pallas_call(
        attention_body,
        out_shape=(
            jax.ShapeDtypeStruct((HEAD_DIM, rows), jnp.bfloat16),
            jax.ShapeDtypeStruct((HEAD_DIM, rows), jnp.float32),
            kv,
            kv,
        ),
        in_specs=[smem] * 3 + [vmem] * 8,
        out_specs=(vmem,) * 4,
        scratch_shapes=[
            pltpu.VMEM((PLANE, BLOCK, rows), jnp.bfloat16),
            pltpu.VMEM((PLANE, 1, rows), jnp.float32),
        ],
        compiler_params=pltpu.CompilerParams(vmem_limit_bytes=VMEM_LIMIT),
        cost_estimate=pl.CostEstimate(
            flops=pairs * HEAD_DIM * 12, bytes_accessed=16 * 1024 * 1024, transcendentals=pairs
        ),
    )(
        scalars,
        key_slots,
        value_slots,
        token,
        lowest,
        query_t,
        query_t.T,
        grad_t,
        grad_t.T,
        keys,
        values,
    )


def rotate_t(values, cosine, sine):
    parts = []
    for start in range(0, values.shape[0], HEAD_DIM):
        upper = values[start : start + HALF]
        lower = values[start + HALF : start + HEAD_DIM]
        parts += [upper * cosine - lower * sine, lower * cosine + upper * sine]
    return jnp.concatenate(parts, axis=0)


def shards(hidden, w_query, w_key, w_value, out_grad, lengths, advantages):
    x, y = lax.axis_index("x"), lax.axis_index("y")
    zl, zh, c = lax.axis_index("zl"), lax.axis_index("zh"), lax.axis_index("c")
    local_tokens, width = hidden.shape
    row_block = w_query.shape[0]
    half_cols = w_query.shape[1] // 2
    pair_cols = 2 * HEAD_DIM

    w_half0 = jnp.concatenate([w_key, w_query[:, :half_cols]], axis=1)
    w_half1 = jnp.concatenate([w_value, w_query[:, half_cols:]], axis=1)
    w_own, w_other = regroup(w_half0, w_half1, zl, c)
    w_rows0, w_rows1 = in_order(w_own, w_other, zl)
    first_cols = HEAD_DIM + pair_cols
    w_first = gather_rows(w_rows0[:, :first_cols], w_rows1[:, :first_cols])
    w_second = gather_rows(w_rows0[:, first_cols:], w_rows1[:, first_cols:])

    z_pairs = []
    for a in range(2):
        for b in range(2):
            for d in range(2):
                z_pairs.append((a * 4 + b * 2 + d, (1 - a) * 4 + (b ^ d) * 2 + d))
    hidden_other = lax.ppermute(hidden, ("zl", "zh", "c"), z_pairs)
    hidden_pair = jnp.concatenate(in_order(hidden, hidden_other, zl), axis=0)

    slot = jnp.arange(2 * PLANE, dtype=jnp.int32)
    inner = slot % PLANE
    slow, fast = inner // SIDE, inner % SIDE
    low = slot < PLANE
    dx, dy = jnp.where(low, fast, slow), jnp.where(low, slow, fast)
    relative = (((x + dx) % SIDE) * SIDE + (y + dy) % SIDE) * 2 + jnp.where(low, 0, 1)
    ax, ay, al = slot // 8, (slot // 2) % SIDE, slot % 2
    rx, ry = (ax - x) % SIDE, (ay - y) % SIDE
    absolute = jnp.where(al == 0, ry * SIDE + rx, PLANE + rx * SIDE + ry)
    hidden_t = permute_blocks(
        hidden_pair.T.reshape(2 * PLANE, row_block, 2 * local_tokens), relative
    ).reshape(width, 2 * local_tokens)
    hidden_rel = hidden_t.T

    block = x * SIDE + y
    tokens = block * BLOCK + jnp.arange(BLOCK, dtype=jnp.int32)
    boundary = jnp.cumsum(lengths)
    segment = jnp.sum((tokens[:, None] >= boundary[None, :]).astype(jnp.int32), axis=1)
    member = segment[:, None] == jnp.arange(lengths.shape[0], dtype=jnp.int32)[None, :]
    start = jnp.sum(jnp.where(member, (boundary - lengths)[None, :], 0), axis=1)
    exponent = jnp.arange(HALF, dtype=jnp.float32) * (2.0 / HEAD_DIM)
    inverse = jnp.exp(-math.log(ROPE_THETA) * exponent)
    angles = inverse[:, None] * (tokens - start).astype(jnp.float32)[None, :]
    cosine, sine = jnp.cos(angles), jnp.sin(angles)
    kv_cosine = jnp.where(c == 0, cosine, 1.0)
    kv_sine = jnp.where(c == 0, sine, 0.0)

    own_tokens = block * BLOCK + zl * local_tokens + jnp.arange(local_tokens, dtype=jnp.int32)
    own_segment = jnp.sum((own_tokens[:, None] >= boundary[None, :]).astype(jnp.int32), axis=1)
    own_member = own_segment[:, None] == jnp.arange(lengths.shape[0], dtype=jnp.int32)[None, :]
    own_advantage = jnp.sum(jnp.where(own_member, advantages[None, :], 0.0), axis=1)
    token_grad = (out_grad.astype(jnp.float32) * own_advantage[:, None]).astype(jnp.bfloat16)
    tg_own, tg_other = regroup(token_grad[:, :half_cols], token_grad[:, half_cols:], zl, c)
    grad_t = jnp.concatenate(in_order(tg_own, tg_other, zl), axis=0).T

    first_t = jnp.dot(hidden_rel, w_first, preferred_element_type=jnp.float32).T
    kv = rotate_t(first_t[:HEAD_DIM], kv_cosine, kv_sine).astype(jnp.bfloat16).T
    query_t0 = rotate_t(first_t[HEAD_DIM:], cosine, sine).astype(jnp.bfloat16)

    line = jnp.stack([kv] + [cross_push(kv, SIDE - s, True) for s in (1, 2, 3)])
    area = jnp.concatenate([line] + [cross_push(line, SIDE - s, False) for s in (1, 2, 3)], axis=0)
    area_other = swap_core(area)
    keys = jnp.where(c == 0, area, area_other)
    values = jnp.where(c == 0, area_other, area)

    second_t = jnp.dot(hidden_rel, w_second, preferred_element_type=jnp.float32).T
    query_t1 = rotate_t(second_t, cosine, sine).astype(jnp.bfloat16)

    blocks = jnp.arange(PLANE, dtype=jnp.int32)
    bx, by = (blocks // SIDE - x) % SIDE, (blocks % SIDE - y) % SIDE
    key_slots = by * SIDE + bx
    value_slots = bx * SIDE + by
    scalars = jnp.stack([start[0] // BLOCK, block, start[BLOCK - 1] // BLOCK]).astype(jnp.int32)
    token_row = jnp.concatenate([tokens, tokens])[None, :]
    lowest_row = jnp.concatenate([start, start])[None, :]

    outs = []
    for pair, query_t in enumerate((query_t0, query_t1)):
        wide = [query_t, grad_t[pair * pair_cols : (pair + 1) * pair_cols]]
        wide = [jnp.concatenate([w[:HEAD_DIM], w[HEAD_DIM:]], axis=1) for w in wide]
        outs.append(
            attention(
                scalars, key_slots, value_slots, token_row, lowest_row, wide[0], wide[1], keys, values
            )
        )
    attended = jnp.concatenate(
        [o[0][:, h * BLOCK : (h + 1) * BLOCK] for o in outs for h in range(2)], axis=0
    ).T
    at0, at1 = attended[:local_tokens], attended[local_tokens:]
    at_halves = ungroup(*in_order(at0, at1, zl), zl, c)
    attended_out = jnp.concatenate(at_halves, axis=1)

    dquery_t = [
        rotate_t(
            jnp.concatenate([o[1][:, :BLOCK], o[1][:, BLOCK:]], axis=0), cosine, -sine
        ).astype(jnp.bfloat16)
        for o in outs
    ]

    dkey = (outs[0][2] + outs[1][2]).astype(jnp.bfloat16)
    dvalue = (outs[0][3] + outs[1][3]).astype(jnp.bfloat16)
    kept = jnp.where(c == 0, dkey, dvalue)
    area = total([kept, swap_core(jnp.where(c == 0, dvalue, dkey))])
    lines = area.reshape(SIDE, SIDE, BLOCK, HEAD_DIM)
    line = total([lines[0]] + [cross_push(lines[s], s, False) for s in (1, 2, 3)])
    dkv = line[0].astype(jnp.float32)
    for s in (1, 2, 3):
        dkv = dkv + cross_push(line[s], s, True).astype(jnp.float32)
    dkv_t = dkv.T * jnp.where(c == 0, SCALE, 1.0)
    dkv_t = rotate_t(dkv_t, kv_cosine, -kv_sine).astype(jnp.bfloat16)

    grad_first = jnp.concatenate([dkv_t, dquery_t[0]], axis=0).T
    grad_second = dquery_t[1].T
    dw = []
    for grad in (grad_second, grad_first):
        term = jnp.dot(hidden_t, grad, preferred_element_type=jnp.float32).astype(jnp.bfloat16)
        dw.append(scatter_rows(term))
    dw_rows = [jnp.concatenate([dw[1][i], dw[0][i]], axis=1) for i in range(2)]
    dw0, dw1 = ungroup(*in_order(dw_rows[0], dw_rows[1], zl), zl, c)
    grad_w_key = dw0[:, :HEAD_DIM]
    grad_w_value = dw1[:, :HEAD_DIM]
    grad_w_query = jnp.concatenate([dw0[:, HEAD_DIM:], dw1[:, HEAD_DIM:]], axis=1)

    w_all = jnp.concatenate([w_first, w_second], axis=1)
    w_all = permute_blocks(w_all.reshape(2 * PLANE, row_block, w_all.shape[1]), absolute)
    w_all = w_all.reshape(width, w_all.shape[-1])
    grad_all = jnp.concatenate([grad_first, grad_second], axis=1)
    dhidden = lax.dot_general(
        grad_all, w_all, (((1,), (1,)), ((), ())), preferred_element_type=jnp.float32
    ).astype(jnp.bfloat16)
    out_cols = width // 4
    tiles = [
        [
            [
                dhidden[a * local_tokens : (a + 1) * local_tokens, (2 * b + d) * out_cols : (2 * b + d + 1) * out_cols]
                for d in range(2)
            ]
            for b in range(2)
        ]
        for a in range(2)
    ]
    stacked = [jnp.stack([tiles[z % 2][z // 2][d] for z in range(4)]) for d in range(2)]
    keep = jnp.where(c == 0, stacked[0], stacked[1])
    give = jnp.where(c == 0, stacked[1], stacked[0])
    chip = total([keep, swap_core(give)])
    z = zh * 2 + zl
    ring = [(0, 0), (1, 0), (0, 1), (1, 1)]
    parts = [lax.dynamic_index_in_dim(chip, z, 0, keepdims=False)]
    for s in (1, 2, 3):
        pairs = [
            (ring[i][0] * 2 + ring[i][1], ring[(i + s) % 4][0] * 2 + ring[(i + s) % 4][1])
            for i in range(4)
        ]
        piece = lax.dynamic_index_in_dim(chip, (z + s) % 4, 0, keepdims=False)
        parts.append(lax.ppermute(piece, ("zl", "zh"), pairs))
    grad_hidden = total(parts)

    return attended_out, grad_hidden, grad_w_query, grad_w_key, grad_w_value


def solution(mesh):
    fine = Mesh(mesh.devices.reshape(SIDE, SIDE, 2, 2, 2), ("x", "y", "zl", "zh", "c"))
    dp, mp = ("x", "y", "zl"), ("zh", "c")
    return jax.shard_map(
        shards,
        mesh=fine,
        in_specs=(P(dp, None), P(dp, mp), P(dp, mp), P(dp, mp), P(dp, mp), P(), P()),
        out_specs=(P(dp, mp),) * 5,
        check_vma=False,
    )
```

```python
import functools
import math

import jax
import jax.numpy as jnp
from jax import lax
from jax.experimental import pallas as pl
from jax.experimental.pallas import tpu as pltpu
from jax.sharding import Mesh, PartitionSpec as P

HEAD_DIM = 128
HALF = 64
ROPE_THETA = 1000000.0
NEG_LARGE = -1e30
SCALE = 1.0 / math.sqrt(HEAD_DIM)
LOG2E = 1.4426950408889634
SIDE = 4
PLANE = SIDE * SIDE
BLOCK = 384


def plane_index(x, y, c):
    return (x * SIDE + y) * 2 + c


def cross_push(value, step, first):
    pairs = []
    for x in range(SIDE):
        for y in range(SIDE):
            for c in range(2):
                along_x = (c == 0) == first
                target = ((x + step) % SIDE, y) if along_x else (x, (y + step) % SIDE)
                pairs.append((plane_index(x, y, c), plane_index(*target, c)))
    return lax.ppermute(value, ("x", "y", "c"), pairs)


def swap_core(value):
    return lax.ppermute(value, "c", [(0, 1), (1, 0)])


ROUND = [(0, 1), (3, 2), (1, 3), (2, 0)]
ROUND_BACK = [(b, a) for a, b in ROUND]
CROSS = [(1, 2), (2, 1)]


def regroup(half0, half1, zl, c):
    first = jnp.where(zl == 0, half0, half1)
    second = jnp.where(zl == 0, half1, half0)
    moved = lax.ppermute(second, ("zl", "c"), ROUND)
    crossed = lax.ppermute(first, ("zl", "c"), CROSS)
    own = jnp.where(zl == c, first, moved)
    other = jnp.where(zl == c, moved, crossed)
    return own, other


def ungroup(own, other, zl, c):
    moved = lax.ppermute(jnp.where(zl == c, other, own), ("zl", "c"), ROUND_BACK)
    crossed = lax.ppermute(other, ("zl", "c"), CROSS)
    first = jnp.where(zl == c, own, crossed)
    half0 = jnp.where(zl == 0, first, moved)
    half1 = jnp.where(zl == 0, moved, first)
    return half0, half1


def in_order(own, other, zl):
    return jnp.where(zl == 0, own, other), jnp.where(zl == 0, other, own)


def total(parts):
    result = parts[0].astype(jnp.float32)
    for part in parts[1:]:
        result = result + part.astype(jnp.float32)
    return result.astype(jnp.bfloat16)


def after(value, others):
    return lax.optimization_barrier((value, others))


VMEM = pl.BlockSpec(memory_space=pltpu.VMEM)
SMEM = pl.BlockSpec(memory_space=pltpu.SMEM)


def call(body, inputs, shapes, scalars=1, limit=24, flops=1, scratch=(), name=None):
    return pl.pallas_call(
        body,
        out_shape=tuple(shapes),
        in_specs=[SMEM] * scalars + [VMEM] * (len(inputs) - scalars),
        out_specs=(VMEM,) * len(shapes),
        scratch_shapes=list(scratch),
        compiler_params=pltpu.CompilerParams(vmem_limit_bytes=limit * 1024 * 1024),
        cost_estimate=pl.CostEstimate(flops=flops, bytes_accessed=1, transcendentals=0),
        name=name,
    )(*inputs)


def block_of(where_ref, far, near):
    along_x = where_ref[3] == 0
    px = (where_ref[0] + jnp.where(along_x, near, far)) % SIDE
    py = (where_ref[1] + jnp.where(along_x, far, near)) % SIDE
    return px * SIDE + py


def turn(value, cosine, sine, sign):
    return value * cosine + pltpu.roll(value, HALF, 1) * (sine * sign)


def transpose_body(where_ref, own_ref, other_ref, result_ref):
    zl = where_ref[2]

    @pl.loop(0, result_ref.shape[0] // HEAD_DIM)
    def _(i):
        spot = pl.ds(pl.multiple_of(i * HEAD_DIM, HEAD_DIM), HEAD_DIM)
        own, other = own_ref[:, spot], other_ref[:, spot]
        low = jnp.where(zl == 0, own, other)
        high = jnp.where(zl == 0, other, own)
        result_ref[spot, :] = jnp.concatenate([low, high], axis=0).T


def project_body(heads, where_ref, *refs):
    strips = refs[:SIDE]
    own_ref, other_ref, cosine_ref, sine_ref = refs[SIDE : SIDE + 4]
    *results, weight_ref = refs[-1 - len(heads) :]
    zl = where_ref[2]
    small = weight_ref.shape[1]
    for far in range(SIDE):
        for near in range(SIDE):
            weight_ref[block_of(where_ref, far, near)] = strips[far][
                near * small : (near + 1) * small, :
            ]
    tokens = own_ref.shape[0]
    blocks = SIDE
    for row, ref in ((zl, own_ref), (1 - zl, other_ref)):
        acc = None
        for k in range(0, PLANE, blocks):
            weight = weight_ref[k : k + blocks].reshape(blocks * small, weight_ref.shape[2])
            part = jnp.dot(
                ref[:, k * small : (k + blocks) * small], weight, preferred_element_type=jnp.float32
            )
            acc = part if acc is None else acc + part
        place = pl.ds(pl.multiple_of(row * tokens, tokens), tokens)
        column = 0
        for (table, count), result_ref in zip(heads, results, strict=True):
            cosine, sine = cosine_ref[table, place, :], sine_ref[table, place, :]
            for h in range(count):
                result_ref[place, h * HEAD_DIM : (h + 1) * HEAD_DIM] = turn(
                    acc[:, column : column + HEAD_DIM], cosine, sine, 1.0
                ).astype(jnp.bfloat16)
                column += HEAD_DIM


def project(heads, where, strips, own, other, cosine, sine):
    cols = strips[0].shape[1]
    width = own.shape[1]
    results = [
        jax.ShapeDtypeStruct((2 * own.shape[0], count * HEAD_DIM), jnp.bfloat16) for _, count in heads
    ]
    return call(
        functools.partial(project_body, heads),
        [where, *strips, own, other, cosine, sine],
        [*results, jax.ShapeDtypeStruct((PLANE, width // PLANE, cols), jnp.bfloat16)],
        name=f"project_{cols}",
    )


def terms_body(where_ref, hidden_ref, grad_ref, *strips):
    small = strips[0].shape[0] // SIDE
    for far in range(SIDE):
        rows = []
        for near in range(SIDE):
            place = pl.multiple_of(block_of(where_ref, far, near) * small, small)
            rows.append(hidden_ref[pl.ds(place, small), :])
        strips[far][...] = jnp.dot(
            jnp.concatenate(rows, axis=0), grad_ref[...], preferred_element_type=jnp.float32
        ).astype(jnp.bfloat16)


def weight_terms(where, hidden_t, grad):
    cols = grad.shape[1]
    strip = jax.ShapeDtypeStruct((hidden_t.shape[0] // SIDE, cols), jnp.bfloat16)
    return call(
        terms_body,
        [where, hidden_t, grad],
        [strip] * SIDE,
        name=f"weight_terms_{cols}",
    )


def input_body(where_ref, dkv_ref, dq0_ref, dq1_ref, first_ref, second_ref, keep_ref, give_ref):
    c = where_ref[3]
    tokens, cols = keep_ref.shape[1:]
    blocks = PLANE // SIDE
    contract = (((1,), (1,)), ((), ()))
    first_grad = jnp.concatenate([dkv_ref[...], dq0_ref[...]], axis=1)
    second_grad = dq1_ref[...]
    for out_ref, core in ((keep_ref, c), (give_ref, 1 - c)):
        for zh in range(2):
            place = pl.ds((2 * zh + core) * blocks, blocks)
            first = first_ref[place].reshape(cols, first_ref.shape[2])
            second = second_ref[place].reshape(cols, second_ref.shape[2])
            tile = lax.dot_general(first_grad, first, contract, preferred_element_type=jnp.float32)
            tile = tile + lax.dot_general(
                second_grad, second, contract, preferred_element_type=jnp.float32
            )
            tile = tile.astype(jnp.bfloat16)
            for zl in range(2):
                out_ref[zh * 2 + zl] = tile[zl * tokens : (zl + 1) * tokens]


def input_terms(where, dkv, dq0, dq1, first, second):
    width = first.shape[0] * first.shape[1]
    out = jax.ShapeDtypeStruct((4, dkv.shape[0] // 2, width // 4), jnp.bfloat16)
    return call(
        input_body,
        [where, dkv, dq0, dq1, first, second],
        [out, out],
        flops=4 * dkv.shape[0] * width * (first.shape[2] + second.shape[2]),
        name="input_terms",
    )


def in_pairs(start, end, step, carry):
    pairs = (end - start) // 2
    carry = lax.fori_loop(
        0, pairs, lambda i, v: step(start + 2 * i + 1, step(start + 2 * i, v)), carry
    )
    return lax.fori_loop(start + 2 * pairs, end, step, carry)


def attention_body(last, scalar_ref, own_slot_ref, other_slot_ref, *refs):
    token_ref, lowest_ref, cosine_ref, sine_ref, query_ref, grad_ref = refs[:6]
    own_refs, other_refs = refs[6 : 6 + SIDE], refs[6 + SIDE : 6 + 2 * SIDE]
    rest = refs[6 + 2 * SIDE :]
    if last:
        before_key_ref, before_value_ref, *rest = rest
        attended_ref, dquery_ref, *rest = rest
        keep_refs, give_refs, scratch = rest[:SIDE], rest[SIDE : 2 * SIDE], rest[2 * SIDE :]
        probs_ref, tops_ref, key_ref, value_ref, dkey_ref, dvalue_ref = scratch
    else:
        attended_ref, dquery_ref, dkey_ref, dvalue_ref, *scratch = rest
        probs_ref, tops_ref, key_ref, value_ref = scratch
    first_block = scalar_ref[0]
    last_block = scalar_ref[1]
    mask_below = scalar_ref[2]
    core = scalar_ref[3]
    rows = 2 * BLOCK
    token = token_ref[...]
    lowest = lowest_ref[...]
    for far in range(SIDE):
        for near in range(SIDE):
            own, other = own_refs[far][near], other_refs[far][near]
            own_block, other_block = own_slot_ref[far * SIDE + near], other_slot_ref[far * SIDE + near]

            @pl.when(core == 0)
            def _():
                key_ref[own_block] = own
                value_ref[other_block] = other

            @pl.when(core == 1)
            def _():
                key_ref[other_block] = other
                value_ref[own_block] = own

    query = jnp.concatenate([query_ref[:, :HEAD_DIM], query_ref[:, HEAD_DIM:]], axis=0)
    grad = jnp.concatenate([grad_ref[:, :HEAD_DIM], grad_ref[:, HEAD_DIM:]], axis=0)
    query_t = query.T
    grad_t = grad.T

    @pl.loop(0, PLANE)
    def _(b):
        dkey_ref[b] = jnp.zeros(dkey_ref.shape[1:], jnp.float32)
        dvalue_ref[b] = jnp.zeros(dvalue_ref.shape[1:], jnp.float32)

    def forward(hide, b, carry):
        top, weight, output = carry
        scores = jnp.dot(key_ref[b], query_t, preferred_element_type=jnp.float32)
        scores = scores * (SCALE * LOG2E)
        if hide:
            position = lax.broadcasted_iota(jnp.int32, scores.shape, 0)
            allowed = (position <= token - b * BLOCK) & (position >= lowest - b * BLOCK)
            scores = jnp.where(allowed, scores, NEG_LARGE)
        new_top = jnp.maximum(top, jnp.max(scores, axis=0, keepdims=True))
        probs = jnp.exp2(scores - new_top)
        fade = jnp.exp2(top - new_top)
        rounded = probs.astype(jnp.bfloat16)
        probs_ref[b] = rounded
        tops_ref[b] = new_top
        weight = weight * fade + jnp.sum(probs, axis=0, keepdims=True)
        output = output * fade + jnp.dot(
            value_ref[b].T, rounded, preferred_element_type=jnp.float32
        )
        return new_top, weight, output

    carry = (
        jnp.full((1, rows), NEG_LARGE, jnp.float32),
        jnp.zeros((1, rows), jnp.float32),
        jnp.zeros((HEAD_DIM, rows), jnp.float32),
    )
    hidden_end = jnp.minimum(mask_below + 1, last_block)
    carry = lax.fori_loop(first_block, hidden_end, functools.partial(forward, True), carry)
    carry = in_pairs(hidden_end, last_block, functools.partial(forward, False), carry)
    top, weight, output = forward(True, last_block, carry)
    inverse = 1.0 / weight
    attended_t = output * inverse
    attended = attended_t.T.astype(jnp.bfloat16)
    attended_ref[:, :HEAD_DIM] = attended[:BLOCK]
    attended_ref[:, HEAD_DIM:] = attended[BLOCK:]
    delta = jnp.sum(
        attended_t.astype(jnp.bfloat16).astype(jnp.float32) * grad_t.astype(jnp.float32),
        axis=0,
        keepdims=True,
    )

    def backward(b, dquery):
        key = key_ref[b]
        prob_grad = jnp.dot(value_ref[b], grad_t, preferred_element_type=jnp.float32)
        probs = probs_ref[b].astype(jnp.float32) * (jnp.exp2(tops_ref[b] - top) * inverse)
        score_grad = (probs * (prob_grad - delta)).astype(jnp.bfloat16)
        dvalue_ref[b] = jnp.dot(
            probs.astype(jnp.bfloat16), grad, preferred_element_type=jnp.float32
        )
        dkey_ref[b] = jnp.dot(score_grad, query, preferred_element_type=jnp.float32)
        return dquery + jnp.dot(key.T, score_grad, preferred_element_type=jnp.float32)

    dquery = in_pairs(
        first_block, last_block + 1, backward, jnp.zeros((HEAD_DIM, rows), jnp.float32)
    )
    dquery = dquery.T * SCALE
    cosine, sine = cosine_ref[...], sine_ref[...]
    for h in range(2):
        dquery_ref[:, h * HEAD_DIM : (h + 1) * HEAD_DIM] = turn(
            dquery[h * BLOCK : (h + 1) * BLOCK], cosine, sine, -1.0
        ).astype(jnp.bfloat16)

    if last:
        for far in range(SIDE):
            for near in range(SIDE):
                slot = far * SIDE + near
                own_block, other_block = own_slot_ref[slot], other_slot_ref[slot]

                @pl.when(core == 0)
                def _():
                    keep_refs[far][near] = (dkey_ref[own_block] + before_key_ref[own_block]).astype(
                        jnp.bfloat16
                    )
                    give_refs[far][near] = (
                        dvalue_ref[other_block] + before_value_ref[other_block]
                    ).astype(jnp.bfloat16)

                @pl.when(core == 1)
                def _():
                    keep_refs[far][near] = (
                        dvalue_ref[own_block] + before_value_ref[own_block]
                    ).astype(jnp.bfloat16)
                    give_refs[far][near] = (dkey_ref[other_block] + before_key_ref[other_block]).astype(
                        jnp.bfloat16
                    )


def attention(scalars, own_slots, other_slots, *inputs, before=()):
    rows = 2 * BLOCK
    query = inputs[4]
    wide = jax.ShapeDtypeStruct(query.shape, jnp.bfloat16)
    area = (PLANE, BLOCK, HEAD_DIM)
    scratch = [
        pltpu.VMEM((PLANE, BLOCK, rows), jnp.bfloat16),
        pltpu.VMEM((PLANE, 1, rows), jnp.float32),
        pltpu.VMEM(area, jnp.bfloat16),
        pltpu.VMEM(area, jnp.bfloat16),
    ]
    if before:
        sums = [jax.ShapeDtypeStruct((SIDE, BLOCK, HEAD_DIM), jnp.bfloat16)] * (2 * SIDE)
        scratch += [pltpu.VMEM(area, jnp.float32)] * 2
    else:
        sums = [jax.ShapeDtypeStruct(area, jnp.float32)] * 2
    return call(
        functools.partial(attention_body, bool(before)),
        [scalars, own_slots, other_slots, *inputs, *before],
        [wide, wide, *sums],
        scalars=3,
        limit=44,
        flops=PLANE * BLOCK * rows * HEAD_DIM * 12,
        scratch=scratch,
        name="attention",
    )


def shards(hidden, w_query, w_key, w_value, out_grad, lengths, advantages):
    x, y = lax.axis_index("x"), lax.axis_index("y")
    zl, zh, c = lax.axis_index("zl"), lax.axis_index("zh"), lax.axis_index("c")
    where = jnp.stack([x, y, zl, c]).astype(jnp.int32)
    local_tokens, width = hidden.shape
    half_cols = w_query.shape[1] // 2

    w_half0 = jnp.concatenate([w_key, w_query[:, :half_cols]], axis=1)
    w_half1 = jnp.concatenate([w_value, w_query[:, half_cols:]], axis=1)
    w_own, w_other = regroup(w_half0, w_half1, zl, c)
    rows_by_half = in_order(w_own, w_other, zl)

    z_pairs = []
    for a in range(2):
        for b in range(2):
            for d in range(2):
                z_pairs.append((a * 4 + b * 2 + d, (1 - a) * 4 + (b ^ d) * 2 + d))
    hidden_later, _ = after(hidden, w_other)
    hidden_other = lax.ppermute(hidden_later, ("zl", "zh", "c"), z_pairs)
    hidden_t = call(
        transpose_body,
        [where, hidden, hidden_other],
        [jax.ShapeDtypeStruct((width, 2 * local_tokens), jnp.bfloat16)],
        name="transpose",
    )[0]
    out_grad, _ = after(out_grad, hidden_other)

    rows = jnp.concatenate(rows_by_half, axis=0)
    pieces = [rows] + [cross_push(rows, SIDE - s, True) for s in (1, 2, 3)]
    first_cols = 3 * HEAD_DIM
    first_line = jnp.concatenate([p[:, :first_cols] for p in pieces], axis=0)
    second_line = jnp.concatenate([p[:, first_cols:] for p in pieces], axis=0)
    first_strips = [first_line] + [cross_push(first_line, SIDE - s, False) for s in (1, 2, 3)]

    block = x * SIDE + y
    tokens = block * BLOCK + jnp.arange(BLOCK, dtype=jnp.int32)
    boundary = jnp.cumsum(lengths)
    segment = jnp.sum((tokens[:, None] >= boundary[None, :]).astype(jnp.int32), axis=1)
    member = segment[:, None] == jnp.arange(lengths.shape[0], dtype=jnp.int32)[None, :]
    start = jnp.sum(jnp.where(member, (boundary - lengths)[None, :], 0), axis=1)
    exponent = jnp.arange(HALF, dtype=jnp.float32) * (2.0 / HEAD_DIM)
    inverse = jnp.exp(-math.log(ROPE_THETA) * exponent)
    angles = (tokens - start).astype(jnp.float32)[:, None] * inverse[None, :]
    cosine, sine = jnp.cos(angles), jnp.sin(angles)
    cosine = jnp.concatenate([cosine, cosine], axis=1)
    sine = jnp.concatenate([-sine, sine], axis=1)
    kv_cosine = jnp.where(c == 0, cosine, 1.0)
    kv_sine = jnp.where(c == 0, sine, 0.0)
    cosines, sines = jnp.stack([kv_cosine, cosine]), jnp.stack([kv_sine, sine])

    own_tokens = block * BLOCK + zl * local_tokens + jnp.arange(local_tokens, dtype=jnp.int32)
    own_segment = jnp.sum((own_tokens[:, None] >= boundary[None, :]).astype(jnp.int32), axis=1)
    own_member = own_segment[:, None] == jnp.arange(lengths.shape[0], dtype=jnp.int32)[None, :]
    own_advantage = jnp.sum(jnp.where(own_member, advantages[None, :], 0.0), axis=1)
    token_grad = (out_grad.astype(jnp.float32) * own_advantage[:, None]).astype(jnp.bfloat16)
    tg_own, tg_other = regroup(token_grad[:, :half_cols], token_grad[:, half_cols:], zl, c)
    grad = jnp.concatenate(in_order(tg_own, tg_other, zl), axis=0)

    kv, query0, w_first = project(
        ((0, 1), (1, 2)), where, first_strips, hidden, hidden_other, cosines, sines
    )
    line = jnp.stack([kv] + [cross_push(kv, SIDE - s, True) for s in (1, 2, 3)])
    line, _ = after(line, hidden_t)
    own_lines = [line] + [cross_push(line, SIDE - s, False) for s in (1, 2, 3)]
    other_lines = [swap_core(v) for v in own_lines]
    second_line, _ = after(second_line, own_lines[1:])
    second_strips = [second_line] + [cross_push(second_line, SIDE - s, False) for s in (1, 2, 3)]

    slots = jnp.arange(PLANE, dtype=jnp.int32)
    far, near = slots // SIDE, slots % SIDE
    x_near = ((x + near) % SIDE) * SIDE + (y + far) % SIDE
    y_near = ((x + far) % SIDE) * SIDE + (y + near) % SIDE
    own_slots = jnp.where(c == 0, x_near, y_near)
    other_slots = jnp.where(c == 0, y_near, x_near)
    scalars = jnp.stack([start[0] // BLOCK, block, start[BLOCK - 1] // BLOCK, c]).astype(jnp.int32)
    token_row = jnp.concatenate([tokens, tokens])[None, :]
    lowest_row = jnp.concatenate([start, start])[None, :]
    pair_cols = 2 * HEAD_DIM

    def attend(query, pair_grad, before=()):
        tables = (token_row, lowest_row, cosine, sine)
        lines = (*own_lines, *other_lines)
        return attention(
            scalars, own_slots, other_slots, *tables, query, pair_grad, *lines, before=before
        )

    attended0, dquery0, *before = attend(query0, grad[:, :pair_cols])
    terms0 = weight_terms(where, hidden_t, dquery0)
    moved0 = [cross_push(terms0[s], s, False) for s in (1, 2, 3)]

    query1, w_second = project(((1, 2),), where, second_strips, hidden, hidden_other, cosines, sines)
    query1, _ = after(query1, terms0[0])
    attended1, dquery1, *sums = attend(query1, grad[:, pair_cols:], before)
    keep, give = sums[:SIDE], after(sums[SIDE:], moved0)[0]
    area = [total([keep[s], swap_core(give[s])]) for s in (1, 2, 3, 0)]
    area = [area[3], *area[:3]]
    line = total([area[0]] + [cross_push(area[s], s, False) for s in (1, 2, 3)])
    dkv = line[0].astype(jnp.float32)
    for s in (1, 2, 3):
        dkv = dkv + cross_push(line[s], s, True).astype(jnp.float32)
    dkv = dkv * jnp.where(c == 0, SCALE, 1.0)
    swapped = jnp.concatenate([dkv[:, HALF:], dkv[:, :HALF]], axis=1)
    dkv = (dkv * kv_cosine - swapped * kv_sine).astype(jnp.bfloat16)

    sum0 = total([terms0[0]] + moved0)
    terms1, _ = after(weight_terms(where, hidden_t, dquery1), area)
    moved1 = [cross_push(terms1[s], s, False) for s in (1, 2, 3)]
    sum1 = total([terms1[0]] + moved1)
    dkv, _ = after(dkv, moved1)
    kv_terms = weight_terms(where, hidden_t, dkv)
    kv_sum = total([kv_terms[0]] + [cross_push(kv_terms[s], s, False) for s in (1, 2, 3)])
    both = jnp.concatenate([kv_sum, sum0, sum1], axis=1)

    keep, give = input_terms(where, after(dkv, kv_terms[0])[0], dquery0, dquery1, w_first, w_second)
    chip = total([keep, swap_core(give)])
    both, _ = after(both, chip)

    attended = jnp.concatenate([attended0, attended1], axis=1)
    attended, _ = after(attended, chip)
    at0, at1 = attended[:local_tokens], attended[local_tokens:]
    attended_out = jnp.concatenate(ungroup(*in_order(at0, at1, zl), zl, c), axis=1)

    small = both.shape[0] // SIDE
    pieces = [both[s * small : (s + 1) * small] for s in range(SIDE)]
    dw_rows = total([pieces[0]] + [cross_push(pieces[s], s, True) for s in (1, 2, 3)])
    dw_rows = dw_rows[: small // 2], dw_rows[small // 2 :]
    dw0, dw1 = ungroup(*in_order(dw_rows[0], dw_rows[1], zl), zl, c)
    grad_w_key = dw0[:, :HEAD_DIM]
    grad_w_value = dw1[:, :HEAD_DIM]
    grad_w_query = jnp.concatenate([dw0[:, HEAD_DIM:], dw1[:, HEAD_DIM:]], axis=1)

    z = zh * 2 + zl
    ring = [(0, 0), (1, 0), (0, 1), (1, 1)]
    parts = [lax.dynamic_index_in_dim(chip, z, 0, keepdims=False)]
    for s in (1, 2, 3):
        pairs = [
            (ring[i][0] * 2 + ring[i][1], ring[(i + s) % 4][0] * 2 + ring[(i + s) % 4][1])
            for i in range(4)
        ]
        piece = lax.dynamic_index_in_dim(chip, (z + s) % 4, 0, keepdims=False)
        parts.append(lax.ppermute(piece, ("zl", "zh"), pairs))
    grad_hidden = total(parts)

    return attended_out, grad_hidden, grad_w_query, grad_w_key, grad_w_value


def solution(mesh):
    fine = Mesh(mesh.devices.reshape(SIDE, SIDE, 2, 2, 2), ("x", "y", "zl", "zh", "c"))
    dp, mp = ("x", "y", "zl"), ("zh", "c")
    return jax.shard_map(
        shards,
        mesh=fine,
        in_specs=(P(dp, None), P(dp, mp), P(dp, mp), P(dp, mp), P(dp, mp), P(), P()),
        out_specs=(P(dp, mp),) * 5,
        check_vma=False,
    )
```

```python
import functools
import math

import jax
import jax.numpy as jnp
from jax import lax
from jax.experimental import pallas as pl
from jax.experimental.pallas import tpu as pltpu
from jax.sharding import Mesh, PartitionSpec as P

HEAD_DIM = 128
HALF = 64
ROPE_THETA = 1000000.0
NEG_LARGE = -1e30
SCALE = 1.0 / math.sqrt(HEAD_DIM)
LOG2E = 1.4426950408889634
SIDE = 4
PLANE = SIDE * SIDE
BLOCK = 384


def plane_index(x, y, c):
    return (x * SIDE + y) * 2 + c


def cross_push(value, step, first):
    pairs = []
    for x in range(SIDE):
        for y in range(SIDE):
            for c in range(2):
                along_x = (c == 0) == first
                target = ((x + step) % SIDE, y) if along_x else (x, (y + step) % SIDE)
                pairs.append((plane_index(x, y, c), plane_index(*target, c)))
    return lax.ppermute(value, ("x", "y", "c"), pairs)


def swap_core(value):
    return lax.ppermute(value, "c", [(0, 1), (1, 0)])


ROUND = [(0, 1), (3, 2), (1, 3), (2, 0)]
ROUND_BACK = [(b, a) for a, b in ROUND]
CROSS = [(1, 2), (2, 1)]


def regroup(half0, half1, zl, c):
    first = jnp.where(zl == 0, half0, half1)
    second = jnp.where(zl == 0, half1, half0)
    moved = lax.ppermute(second, ("zl", "c"), ROUND)
    crossed = lax.ppermute(first, ("zl", "c"), CROSS)
    own = jnp.where(zl == c, first, moved)
    other = jnp.where(zl == c, moved, crossed)
    return own, other


def ungroup(own, other, zl, c):
    moved = lax.ppermute(jnp.where(zl == c, other, own), ("zl", "c"), ROUND_BACK)
    crossed = lax.ppermute(other, ("zl", "c"), CROSS)
    first = jnp.where(zl == c, own, crossed)
    half0 = jnp.where(zl == 0, first, moved)
    half1 = jnp.where(zl == 0, moved, first)
    return half0, half1


def in_order(own, other, zl):
    return jnp.where(zl == 0, own, other), jnp.where(zl == 0, other, own)


def total(parts):
    result = parts[0].astype(jnp.float32)
    for part in parts[1:]:
        result = result + part.astype(jnp.float32)
    return result.astype(jnp.bfloat16)


def after(value, others):
    return lax.optimization_barrier((value, others))


VMEM = pl.BlockSpec(memory_space=pltpu.VMEM)
SMEM = pl.BlockSpec(memory_space=pltpu.SMEM)


def call(body, inputs, shapes, scalars=1, limit=24, flops=1, scratch=(), name=None):
    return pl.pallas_call(
        body,
        out_shape=tuple(shapes),
        in_specs=[SMEM] * scalars + [VMEM] * (len(inputs) - scalars),
        out_specs=(VMEM,) * len(shapes),
        scratch_shapes=list(scratch),
        compiler_params=pltpu.CompilerParams(vmem_limit_bytes=limit * 1024 * 1024),
        cost_estimate=pl.CostEstimate(flops=flops, bytes_accessed=1, transcendentals=0),
        name=name,
    )(*inputs)


def block_of(where_ref, far, near):
    along_x = where_ref[3] == 0
    px = (where_ref[0] + jnp.where(along_x, near, far)) % SIDE
    py = (where_ref[1] + jnp.where(along_x, far, near)) % SIDE
    return px * SIDE + py


def turn(value, cosine, sine, sign):
    return value * cosine + pltpu.roll(value, HALF, 1) * (sine * sign)


def transpose_body(where_ref, own_ref, other_ref, result_ref):
    zl = where_ref[2]

    @pl.loop(0, result_ref.shape[0] // HEAD_DIM)
    def _(i):
        spot = pl.ds(pl.multiple_of(i * HEAD_DIM, HEAD_DIM), HEAD_DIM)
        own, other = own_ref[:, spot], other_ref[:, spot]
        low = jnp.where(zl == 0, own, other)
        high = jnp.where(zl == 0, other, own)
        result_ref[spot, :] = jnp.concatenate([low, high], axis=0).T


def project_body(heads, where_ref, *refs):
    strips = refs[:SIDE]
    own_ref, other_ref, cosine_ref, sine_ref = refs[SIDE : SIDE + 4]
    *results, weight_ref = refs[-1 - len(heads) :]
    zl = where_ref[2]
    small = weight_ref.shape[1]
    for far in range(SIDE):
        for near in range(SIDE):
            weight_ref[block_of(where_ref, far, near)] = strips[far][
                near * small : (near + 1) * small, :
            ]
    tokens = own_ref.shape[0]
    blocks = SIDE
    for row, ref in ((zl, own_ref), (1 - zl, other_ref)):
        acc = None
        for k in range(0, PLANE, blocks):
            weight = weight_ref[k : k + blocks].reshape(blocks * small, weight_ref.shape[2])
            part = jnp.dot(
                ref[:, k * small : (k + blocks) * small], weight, preferred_element_type=jnp.float32
            )
            acc = part if acc is None else acc + part
        place = pl.ds(pl.multiple_of(row * tokens, tokens), tokens)
        column = 0
        for (table, count), result_ref in zip(heads, results, strict=True):
            cosine, sine = cosine_ref[table, place, :], sine_ref[table, place, :]
            for h in range(count):
                result_ref[place, h * HEAD_DIM : (h + 1) * HEAD_DIM] = turn(
                    acc[:, column : column + HEAD_DIM], cosine, sine, 1.0
                ).astype(jnp.bfloat16)
                column += HEAD_DIM


def project(heads, where, strips, own, other, cosine, sine):
    cols = strips[0].shape[1]
    width = own.shape[1]
    results = [
        jax.ShapeDtypeStruct((2 * own.shape[0], count * HEAD_DIM), jnp.bfloat16) for _, count in heads
    ]
    return call(
        functools.partial(project_body, heads),
        [where, *strips, own, other, cosine, sine],
        [*results, jax.ShapeDtypeStruct((PLANE, width // PLANE, cols), jnp.bfloat16)],
        name=f"project_{cols}",
    )


def terms_body(where_ref, hidden_ref, grad_ref, *strips):
    small = strips[0].shape[0] // SIDE
    for far in range(SIDE):
        rows = []
        for near in range(SIDE):
            place = pl.multiple_of(block_of(where_ref, far, near) * small, small)
            rows.append(hidden_ref[pl.ds(place, small), :])
        strips[far][...] = jnp.dot(
            jnp.concatenate(rows, axis=0), grad_ref[...], preferred_element_type=jnp.float32
        ).astype(jnp.bfloat16)


def weight_terms(where, hidden_t, grad):
    cols = grad.shape[1]
    strip = jax.ShapeDtypeStruct((hidden_t.shape[0] // SIDE, cols), jnp.bfloat16)
    return call(
        terms_body,
        [where, hidden_t, grad],
        [strip] * SIDE,
        name=f"weight_terms_{cols}",
    )


def input_body(where_ref, dkv_ref, dq0_ref, dq1_ref, first_ref, second_ref, keep_ref, give_ref):
    c = where_ref[3]
    tokens, cols = keep_ref.shape[1:]
    blocks = PLANE // SIDE
    contract = (((1,), (1,)), ((), ()))
    first_grad = jnp.concatenate([dkv_ref[...], dq0_ref[...]], axis=1)
    second_grad = dq1_ref[...]
    for out_ref, core in ((keep_ref, c), (give_ref, 1 - c)):
        for zh in range(2):
            place = pl.ds((2 * zh + core) * blocks, blocks)
            first = first_ref[place].reshape(cols, first_ref.shape[2])
            second = second_ref[place].reshape(cols, second_ref.shape[2])
            tile = lax.dot_general(first_grad, first, contract, preferred_element_type=jnp.float32)
            tile = tile + lax.dot_general(
                second_grad, second, contract, preferred_element_type=jnp.float32
            )
            tile = tile.astype(jnp.bfloat16)
            for zl in range(2):
                out_ref[zh * 2 + zl] = tile[zl * tokens : (zl + 1) * tokens]


def input_terms(where, dkv, dq0, dq1, first, second):
    width = first.shape[0] * first.shape[1]
    out = jax.ShapeDtypeStruct((4, dkv.shape[0] // 2, width // 4), jnp.bfloat16)
    return call(
        input_body,
        [where, dkv, dq0, dq1, first, second],
        [out, out],
        flops=4 * dkv.shape[0] * width * (first.shape[2] + second.shape[2]),
        name="input_terms",
    )


def in_pairs(start, end, step, carry):
    pairs = (end - start) // 2
    carry = lax.fori_loop(0, pairs, lambda i, v: step(2, start + 2 * i, v), carry)
    return lax.fori_loop(start + 2 * pairs, end, functools.partial(step, 1), carry)


def attention_body(last, scalar_ref, own_slot_ref, other_slot_ref, *refs):
    token_ref, lowest_ref, cosine_ref, sine_ref, query_ref, grad_ref = refs[:6]
    own_refs, other_refs = refs[6 : 6 + SIDE], refs[6 + SIDE : 6 + 2 * SIDE]
    rest = refs[6 + 2 * SIDE :]
    if last:
        before_key_ref, before_value_ref, *rest = rest
        attended_ref, dquery_ref, *rest = rest
        keep_refs, give_refs, scratch = rest[:SIDE], rest[SIDE : 2 * SIDE], rest[2 * SIDE :]
        probs_ref, tops_ref, key_ref, value_ref, dkey_ref, dvalue_ref = scratch
    else:
        attended_ref, dquery_ref, dkey_ref, dvalue_ref, *scratch = rest
        probs_ref, tops_ref, key_ref, value_ref = scratch
    first_block = scalar_ref[0]
    last_block = scalar_ref[1]
    mask_below = scalar_ref[2]
    core = scalar_ref[3]
    rows = 2 * BLOCK
    token = token_ref[...]
    lowest = lowest_ref[...]
    for far in range(SIDE):
        for near in range(SIDE):
            own, other = own_refs[far][near], other_refs[far][near]
            own_block, other_block = own_slot_ref[far * SIDE + near], other_slot_ref[far * SIDE + near]

            @pl.when(core == 0)
            def _():
                key_ref[own_block] = own
                value_ref[other_block] = other

            @pl.when(core == 1)
            def _():
                key_ref[other_block] = other
                value_ref[own_block] = own

    query = jnp.concatenate([query_ref[:, :HEAD_DIM], query_ref[:, HEAD_DIM:]], axis=0)
    grad = jnp.concatenate([grad_ref[:, :HEAD_DIM], grad_ref[:, HEAD_DIM:]], axis=0)
    query_t = query.T
    grad_t = grad.T

    def clear(b):
        dkey_ref[b] = jnp.zeros(dkey_ref.shape[1:], dkey_ref.dtype)
        dvalue_ref[b] = jnp.zeros(dvalue_ref.shape[1:], dvalue_ref.dtype)

    pl.loop(0, first_block)(clear)
    pl.loop(last_block + 1, PLANE)(clear)

    def forward(hide, count, b, carry):
        top, weight, output = carry
        some = pl.ds(b, count)
        keys = key_ref[some].reshape(count * BLOCK, HEAD_DIM)
        scores = jnp.dot(keys, query_t, preferred_element_type=jnp.float32)
        scores = scores * (SCALE * LOG2E)
        if hide:
            position = lax.broadcasted_iota(jnp.int32, scores.shape, 0)
            allowed = (position <= token - b * BLOCK) & (position >= lowest - b * BLOCK)
            scores = jnp.where(allowed, scores, NEG_LARGE)
        new_top = jnp.maximum(top, jnp.max(scores, axis=0, keepdims=True))
        probs = jnp.exp2(scores - new_top)
        fade = jnp.exp2(top - new_top)
        rounded = probs.astype(jnp.bfloat16)
        probs_ref[some] = rounded.reshape(count, BLOCK, rows)
        tops_ref[some] = jnp.broadcast_to(new_top[None], (count, 1, rows))
        weight = weight * fade + jnp.sum(probs, axis=0, keepdims=True)
        values_t = value_ref[some].reshape(count * BLOCK, HEAD_DIM).T
        output = output * fade + jnp.dot(values_t, rounded, preferred_element_type=jnp.float32)
        return new_top, weight, output

    carry = (
        jnp.full((1, rows), NEG_LARGE, jnp.float32),
        jnp.zeros((1, rows), jnp.float32),
        jnp.zeros((HEAD_DIM, rows), jnp.float32),
    )
    hidden_end = jnp.minimum(mask_below + 1, last_block)
    carry = lax.fori_loop(first_block, hidden_end, functools.partial(forward, True, 1), carry)
    carry = in_pairs(hidden_end, last_block, functools.partial(forward, False), carry)
    top, weight, output = forward(True, 1, last_block, carry)
    inverse = 1.0 / weight
    attended_t = output * inverse
    attended = attended_t.T.astype(jnp.bfloat16)
    attended_ref[:, :HEAD_DIM] = attended[:BLOCK]
    attended_ref[:, HEAD_DIM:] = attended[BLOCK:]
    delta = jnp.sum(
        attended_t.astype(jnp.bfloat16).astype(jnp.float32) * grad_t.astype(jnp.float32),
        axis=0,
        keepdims=True,
    )

    def backward(count, b, dquery):
        some = pl.ds(b, count)
        keys = key_ref[some].reshape(count * BLOCK, HEAD_DIM)
        values = value_ref[some].reshape(count * BLOCK, HEAD_DIM)
        prob_grad = jnp.dot(values, grad_t, preferred_element_type=jnp.float32)
        fades = jnp.exp2(tops_ref[some] - top) * inverse
        probs = probs_ref[some].astype(jnp.float32) * fades
        probs = probs.reshape(count * BLOCK, rows)
        score_grad = (probs * (prob_grad - delta)).astype(jnp.bfloat16)
        area = (count, BLOCK, HEAD_DIM)
        dvalue_ref[some] = jnp.dot(
            probs.astype(jnp.bfloat16), grad, preferred_element_type=jnp.float32
        ).reshape(area).astype(dvalue_ref.dtype)
        dkey_ref[some] = jnp.dot(
            score_grad, query, preferred_element_type=jnp.float32
        ).reshape(area).astype(dkey_ref.dtype)
        return dquery + jnp.dot(keys.T, score_grad, preferred_element_type=jnp.float32)

    dquery = in_pairs(
        first_block, last_block + 1, backward, jnp.zeros((HEAD_DIM, rows), jnp.float32)
    )
    dquery = dquery.T * SCALE
    cosine, sine = cosine_ref[...], sine_ref[...]
    for h in range(2):
        dquery_ref[:, h * HEAD_DIM : (h + 1) * HEAD_DIM] = turn(
            dquery[h * BLOCK : (h + 1) * BLOCK], cosine, sine, -1.0
        ).astype(jnp.bfloat16)

    if last:
        for far in range(SIDE):
            for near in range(SIDE):
                slot = far * SIDE + near
                own_block, other_block = own_slot_ref[slot], other_slot_ref[slot]

                @pl.when(core == 0)
                def _():
                    keep_refs[far][near] = (dkey_ref[own_block] + before_key_ref[own_block]).astype(
                        jnp.bfloat16
                    )
                    give_refs[far][near] = (
                        dvalue_ref[other_block] + before_value_ref[other_block]
                    ).astype(jnp.bfloat16)

                @pl.when(core == 1)
                def _():
                    keep_refs[far][near] = (
                        dvalue_ref[own_block] + before_value_ref[own_block]
                    ).astype(jnp.bfloat16)
                    give_refs[far][near] = (dkey_ref[other_block] + before_key_ref[other_block]).astype(
                        jnp.bfloat16
                    )


def attention(scalars, own_slots, other_slots, *inputs, before=()):
    rows = 2 * BLOCK
    query = inputs[4]
    wide = jax.ShapeDtypeStruct(query.shape, jnp.bfloat16)
    area = (PLANE, BLOCK, HEAD_DIM)
    scratch = [
        pltpu.VMEM((PLANE, BLOCK, rows), jnp.bfloat16),
        pltpu.VMEM((PLANE, 1, rows), jnp.float32),
        pltpu.VMEM(area, jnp.bfloat16),
        pltpu.VMEM(area, jnp.bfloat16),
    ]
    if before:
        sums = [jax.ShapeDtypeStruct((SIDE, BLOCK, HEAD_DIM), jnp.bfloat16)] * (2 * SIDE)
        scratch += [pltpu.VMEM(area, jnp.float32)] * 2
    else:
        sums = [jax.ShapeDtypeStruct(area, jnp.bfloat16)] * 2
    return call(
        functools.partial(attention_body, bool(before)),
        [scalars, own_slots, other_slots, *inputs, *before],
        [wide, wide, *sums],
        scalars=3,
        limit=44,
        flops=PLANE * BLOCK * rows * HEAD_DIM * 12,
        scratch=scratch,
        name="attention",
    )


def shards(hidden, w_query, w_key, w_value, out_grad, lengths, advantages):
    x, y = lax.axis_index("x"), lax.axis_index("y")
    zl, zh, c = lax.axis_index("zl"), lax.axis_index("zh"), lax.axis_index("c")
    where = jnp.stack([x, y, zl, c]).astype(jnp.int32)
    local_tokens, width = hidden.shape
    half_cols = w_query.shape[1] // 2

    w_half0 = jnp.concatenate([w_key, w_query[:, :half_cols]], axis=1)
    w_half1 = jnp.concatenate([w_value, w_query[:, half_cols:]], axis=1)
    w_own, w_other = regroup(w_half0, w_half1, zl, c)
    rows_by_half = in_order(w_own, w_other, zl)

    z_pairs = []
    for a in range(2):
        for b in range(2):
            for d in range(2):
                z_pairs.append((a * 4 + b * 2 + d, (1 - a) * 4 + (b ^ d) * 2 + d))
    hidden_later, _ = after(hidden, w_other)
    hidden_other = lax.ppermute(hidden_later, ("zl", "zh", "c"), z_pairs)
    hidden_t = call(
        transpose_body,
        [where, hidden, hidden_other],
        [jax.ShapeDtypeStruct((width, 2 * local_tokens), jnp.bfloat16)],
        name="transpose",
    )[0]
    out_grad, _ = after(out_grad, hidden_other)

    rows = jnp.concatenate(rows_by_half, axis=0)
    pieces = [rows] + [cross_push(rows, SIDE - s, True) for s in (1, 2, 3)]
    first_cols = 3 * HEAD_DIM
    first_line = jnp.concatenate([p[:, :first_cols] for p in pieces], axis=0)
    second_line = jnp.concatenate([p[:, first_cols:] for p in pieces], axis=0)
    first_strips = [first_line] + [cross_push(first_line, SIDE - s, False) for s in (1, 2, 3)]

    block = x * SIDE + y
    tokens = block * BLOCK + jnp.arange(BLOCK, dtype=jnp.int32)
    boundary = jnp.cumsum(lengths)
    segment = jnp.sum((tokens[:, None] >= boundary[None, :]).astype(jnp.int32), axis=1)
    member = segment[:, None] == jnp.arange(lengths.shape[0], dtype=jnp.int32)[None, :]
    start = jnp.sum(jnp.where(member, (boundary - lengths)[None, :], 0), axis=1)
    exponent = jnp.arange(HALF, dtype=jnp.float32) * (2.0 / HEAD_DIM)
    inverse = jnp.exp(-math.log(ROPE_THETA) * exponent)
    angles = (tokens - start).astype(jnp.float32)[:, None] * inverse[None, :]
    cosine, sine = jnp.cos(angles), jnp.sin(angles)
    cosine = jnp.concatenate([cosine, cosine], axis=1)
    sine = jnp.concatenate([-sine, sine], axis=1)
    kv_cosine = jnp.where(c == 0, cosine, 1.0)
    kv_sine = jnp.where(c == 0, sine, 0.0)
    cosines, sines = jnp.stack([kv_cosine, cosine]), jnp.stack([kv_sine, sine])

    own_tokens = block * BLOCK + zl * local_tokens + jnp.arange(local_tokens, dtype=jnp.int32)
    own_segment = jnp.sum((own_tokens[:, None] >= boundary[None, :]).astype(jnp.int32), axis=1)
    own_member = own_segment[:, None] == jnp.arange(lengths.shape[0], dtype=jnp.int32)[None, :]
    own_advantage = jnp.sum(jnp.where(own_member, advantages[None, :], 0.0), axis=1)
    token_grad = (out_grad.astype(jnp.float32) * own_advantage[:, None]).astype(jnp.bfloat16)
    tg_own, tg_other = regroup(token_grad[:, :half_cols], token_grad[:, half_cols:], zl, c)
    grad = jnp.concatenate(in_order(tg_own, tg_other, zl), axis=0)

    kv, query0, w_first = project(
        ((0, 1), (1, 2)), where, first_strips, hidden, hidden_other, cosines, sines
    )
    line = jnp.stack([kv] + [cross_push(kv, SIDE - s, True) for s in (1, 2, 3)])
    line, _ = after(line, hidden_t)
    own_lines = [line] + [cross_push(line, SIDE - s, False) for s in (1, 2, 3)]
    other_lines = [swap_core(v) for v in own_lines]
    second_line, _ = after(second_line, own_lines[1:])
    second_strips = [second_line] + [cross_push(second_line, SIDE - s, False) for s in (1, 2, 3)]

    slots = jnp.arange(PLANE, dtype=jnp.int32)
    far, near = slots // SIDE, slots % SIDE
    x_near = ((x + near) % SIDE) * SIDE + (y + far) % SIDE
    y_near = ((x + far) % SIDE) * SIDE + (y + near) % SIDE
    own_slots = jnp.where(c == 0, x_near, y_near)
    other_slots = jnp.where(c == 0, y_near, x_near)
    scalars = jnp.stack([start[0] // BLOCK, block, start[BLOCK - 1] // BLOCK, c]).astype(jnp.int32)
    token_row = jnp.concatenate([tokens, tokens])[None, :]
    lowest_row = jnp.concatenate([start, start])[None, :]
    pair_cols = 2 * HEAD_DIM

    def attend(query, pair_grad, before=()):
        tables = (token_row, lowest_row, cosine, sine)
        lines = (*own_lines, *other_lines)
        return attention(
            scalars, own_slots, other_slots, *tables, query, pair_grad, *lines, before=before
        )

    attended0, dquery0, *before = attend(query0, grad[:, :pair_cols])
    terms0 = weight_terms(where, hidden_t, dquery0)
    moved0 = [cross_push(terms0[s], s, False) for s in (1, 2, 3)]

    query1, w_second = project(((1, 2),), where, second_strips, hidden, hidden_other, cosines, sines)
    query1, _ = after(query1, terms0[0])
    attended1, dquery1, *sums = attend(query1, grad[:, pair_cols:], before)
    keep, give = sums[:SIDE], after(sums[SIDE:], moved0)[0]
    area = [total([keep[s], swap_core(give[s])]) for s in (1, 2, 3, 0)]
    area = [area[3], *area[:3]]
    line = total([area[0]] + [cross_push(area[s], s, False) for s in (1, 2, 3)])
    dkv = line[0].astype(jnp.float32)
    for s in (1, 2, 3):
        dkv = dkv + cross_push(line[s], s, True).astype(jnp.float32)
    dkv = dkv * jnp.where(c == 0, SCALE, 1.0)
    swapped = jnp.concatenate([dkv[:, HALF:], dkv[:, :HALF]], axis=1)
    dkv = (dkv * kv_cosine - swapped * kv_sine).astype(jnp.bfloat16)

    sum0 = total([terms0[0]] + moved0)
    terms1, _ = after(weight_terms(where, hidden_t, dquery1), area)
    moved1 = [cross_push(terms1[s], s, False) for s in (1, 2, 3)]
    sum1 = total([terms1[0]] + moved1)
    attended = jnp.concatenate([attended0, attended1], axis=1)
    attended, _ = after(attended, dkv)
    at0, at1 = attended[:local_tokens], attended[local_tokens:]
    halves = ungroup(*in_order(at0, at1, zl), zl, c)
    attended_out = jnp.concatenate(halves, axis=1)
    dkv, _ = after(dkv, (moved1[0], halves))
    kv_terms = weight_terms(where, hidden_t, dkv)
    kv_sum = total([kv_terms[0]] + [cross_push(kv_terms[s], s, False) for s in (1, 2, 3)])
    both = jnp.concatenate([kv_sum, sum0, sum1], axis=1)

    keep, give = input_terms(where, after(dkv, kv_terms[0])[0], dquery0, dquery1, w_first, w_second)
    chip = total([keep, swap_core(give)])
    both, _ = after(both, chip)

    small = both.shape[0] // SIDE
    pieces = [both[s * small : (s + 1) * small] for s in range(SIDE)]
    dw_rows = total([pieces[0]] + [cross_push(pieces[s], s, True) for s in (1, 2, 3)])
    dw_rows = dw_rows[: small // 2], dw_rows[small // 2 :]
    dw0, dw1 = ungroup(*in_order(dw_rows[0], dw_rows[1], zl), zl, c)
    grad_w_key = dw0[:, :HEAD_DIM]
    grad_w_value = dw1[:, :HEAD_DIM]
    grad_w_query = jnp.concatenate([dw0[:, HEAD_DIM:], dw1[:, HEAD_DIM:]], axis=1)

    z = zh * 2 + zl
    ring = [(0, 0), (1, 0), (0, 1), (1, 1)]
    parts = [lax.dynamic_index_in_dim(chip, z, 0, keepdims=False)]
    for s in (1, 2, 3):
        pairs = [
            (ring[i][0] * 2 + ring[i][1], ring[(i + s) % 4][0] * 2 + ring[(i + s) % 4][1])
            for i in range(4)
        ]
        piece = lax.dynamic_index_in_dim(chip, (z + s) % 4, 0, keepdims=False)
        parts.append(lax.ppermute(piece, ("zl", "zh"), pairs))
    grad_hidden = total(parts)

    return attended_out, grad_hidden, grad_w_query, grad_w_key, grad_w_value


def solution(mesh):
    fine = Mesh(mesh.devices.reshape(SIDE, SIDE, 2, 2, 2), ("x", "y", "zl", "zh", "c"))
    dp, mp = ("x", "y", "zl"), ("zh", "c")
    return jax.shard_map(
        shards,
        mesh=fine,
        in_specs=(P(dp, None), P(dp, mp), P(dp, mp), P(dp, mp), P(dp, mp), P(), P()),
        out_specs=(P(dp, mp),) * 5,
        check_vma=False,
    )
```

```python
import functools
import math

import jax
import jax.numpy as jnp
from jax import lax
from jax.experimental import pallas as pl
from jax.experimental.pallas import tpu as pltpu
from jax.sharding import Mesh, PartitionSpec as P

HEAD_DIM = 128
HALF = 64
ROPE_THETA = 1000000.0
NEG_LARGE = -1e30
SCALE = 1.0 / math.sqrt(HEAD_DIM)
LOG2E = 1.4426950408889634
SIDE = 4
PLANE = SIDE * SIDE
BLOCK = 384


def plane_index(x, y, c):
    return (x * SIDE + y) * 2 + c


def cross_push(value, step, first):
    pairs = []
    for x in range(SIDE):
        for y in range(SIDE):
            for c in range(2):
                along_x = (c == 0) == first
                target = ((x + step) % SIDE, y) if along_x else (x, (y + step) % SIDE)
                pairs.append((plane_index(x, y, c), plane_index(*target, c)))
    return lax.ppermute(value, ("x", "y", "c"), pairs)


def swap_core(value):
    return lax.ppermute(value, "c", [(0, 1), (1, 0)])


ROUND = [(0, 1), (3, 2), (1, 3), (2, 0)]
ROUND_BACK = [(b, a) for a, b in ROUND]
CROSS = [(1, 2), (2, 1)]


def regroup(half0, half1, zl, c):
    first = jnp.where(zl == 0, half0, half1)
    second = jnp.where(zl == 0, half1, half0)
    moved = lax.ppermute(second, ("zl", "c"), ROUND)
    crossed = lax.ppermute(first, ("zl", "c"), CROSS)
    own = jnp.where(zl == c, first, moved)
    other = jnp.where(zl == c, moved, crossed)
    return own, other


def ungroup(own, other, zl, c):
    moved = lax.ppermute(jnp.where(zl == c, other, own), ("zl", "c"), ROUND_BACK)
    crossed = lax.ppermute(other, ("zl", "c"), CROSS)
    first = jnp.where(zl == c, own, crossed)
    half0 = jnp.where(zl == 0, first, moved)
    half1 = jnp.where(zl == 0, moved, first)
    return half0, half1


def in_order(own, other, zl):
    return jnp.where(zl == 0, own, other), jnp.where(zl == 0, other, own)


def total(parts):
    result = parts[0].astype(jnp.float32)
    for part in parts[1:]:
        result = result + part.astype(jnp.float32)
    return result.astype(jnp.bfloat16)


def after(value, others):
    return lax.optimization_barrier((value, others))


VMEM = pl.BlockSpec(memory_space=pltpu.VMEM)
SMEM = pl.BlockSpec(memory_space=pltpu.SMEM)


def call(body, inputs, shapes, scalars=1, limit=24, flops=1, scratch=(), name=None):
    return pl.pallas_call(
        body,
        out_shape=tuple(shapes),
        in_specs=[SMEM] * scalars + [VMEM] * (len(inputs) - scalars),
        out_specs=(VMEM,) * len(shapes),
        scratch_shapes=list(scratch),
        compiler_params=pltpu.CompilerParams(vmem_limit_bytes=limit * 1024 * 1024),
        cost_estimate=pl.CostEstimate(flops=flops, bytes_accessed=1, transcendentals=0),
        name=name,
    )(*inputs)


def block_of(where_ref, far, near):
    along_x = where_ref[3] == 0
    px = (where_ref[0] + jnp.where(along_x, near, far)) % SIDE
    py = (where_ref[1] + jnp.where(along_x, far, near)) % SIDE
    return px * SIDE + py


def turn(value, cosine, sine, sign):
    return value * cosine + pltpu.roll(value, HALF, 1) * (sine * sign)


def transpose_body(where_ref, own_ref, other_ref, result_ref):
    zl = where_ref[2]

    @pl.loop(0, result_ref.shape[0] // HEAD_DIM)
    def _(i):
        spot = pl.ds(pl.multiple_of(i * HEAD_DIM, HEAD_DIM), HEAD_DIM)
        own, other = own_ref[:, spot], other_ref[:, spot]
        low = jnp.where(zl == 0, own, other)
        high = jnp.where(zl == 0, other, own)
        result_ref[spot, :] = jnp.concatenate([low, high], axis=0).T


def project_body(heads, where_ref, *refs):
    strips = refs[:SIDE]
    own_ref, other_ref, cosine_ref, sine_ref = refs[SIDE : SIDE + 4]
    *results, weight_ref = refs[-1 - len(heads) :]
    zl = where_ref[2]
    small = weight_ref.shape[1]
    for far in range(SIDE):
        for near in range(SIDE):
            weight_ref[block_of(where_ref, far, near)] = strips[far][
                near * small : (near + 1) * small, :
            ]
    tokens = own_ref.shape[0]
    blocks = SIDE
    for row, ref in ((zl, own_ref), (1 - zl, other_ref)):
        acc = None
        for k in range(0, PLANE, blocks):
            weight = weight_ref[k : k + blocks].reshape(blocks * small, weight_ref.shape[2])
            part = jnp.dot(
                ref[:, k * small : (k + blocks) * small], weight, preferred_element_type=jnp.float32
            )
            acc = part if acc is None else acc + part
        place = pl.ds(pl.multiple_of(row * tokens, tokens), tokens)
        column = 0
        for (table, count), result_ref in zip(heads, results, strict=True):
            cosine, sine = cosine_ref[table, place, :], sine_ref[table, place, :]
            for h in range(count):
                result_ref[place, h * HEAD_DIM : (h + 1) * HEAD_DIM] = turn(
                    acc[:, column : column + HEAD_DIM], cosine, sine, 1.0
                ).astype(jnp.bfloat16)
                column += HEAD_DIM


def project(heads, where, strips, own, other, cosine, sine):
    cols = strips[0].shape[1]
    width = own.shape[1]
    results = [
        jax.ShapeDtypeStruct((2 * own.shape[0], count * HEAD_DIM), jnp.bfloat16) for _, count in heads
    ]
    return call(
        functools.partial(project_body, heads),
        [where, *strips, own, other, cosine, sine],
        [*results, jax.ShapeDtypeStruct((PLANE, width // PLANE, cols), jnp.bfloat16)],
        name=f"project_{cols}",
    )


def terms_body(where_ref, hidden_ref, grad_ref, *strips):
    small = strips[0].shape[0] // SIDE
    for far in range(SIDE):
        rows = []
        for near in range(SIDE):
            place = pl.multiple_of(block_of(where_ref, far, near) * small, small)
            rows.append(hidden_ref[pl.ds(place, small), :])
        strips[far][...] = jnp.dot(
            jnp.concatenate(rows, axis=0), grad_ref[...], preferred_element_type=jnp.float32
        ).astype(jnp.bfloat16)


def weight_terms(where, hidden_t, grad):
    cols = grad.shape[1]
    strip = jax.ShapeDtypeStruct((hidden_t.shape[0] // SIDE, cols), jnp.bfloat16)
    return call(
        terms_body,
        [where, hidden_t, grad],
        [strip] * SIDE,
        name=f"weight_terms_{cols}",
    )


def input_body(where_ref, dkv_ref, dq0_ref, dq1_ref, first_ref, second_ref, keep_ref, give_ref):
    c = where_ref[3]
    tokens, cols = keep_ref.shape[1:]
    blocks = PLANE // SIDE
    contract = (((1,), (1,)), ((), ()))
    first_grad = jnp.concatenate([dkv_ref[...], dq0_ref[...]], axis=1)
    second_grad = dq1_ref[...]
    for out_ref, core in ((keep_ref, c), (give_ref, 1 - c)):
        for zh in range(2):
            place = pl.ds((2 * zh + core) * blocks, blocks)
            first = first_ref[place].reshape(cols, first_ref.shape[2])
            second = second_ref[place].reshape(cols, second_ref.shape[2])
            tile = lax.dot_general(first_grad, first, contract, preferred_element_type=jnp.float32)
            tile = tile + lax.dot_general(
                second_grad, second, contract, preferred_element_type=jnp.float32
            )
            tile = tile.astype(jnp.bfloat16)
            for zl in range(2):
                out_ref[zh * 2 + zl] = tile[zl * tokens : (zl + 1) * tokens]


def input_terms(where, dkv, dq0, dq1, first, second):
    width = first.shape[0] * first.shape[1]
    out = jax.ShapeDtypeStruct((4, dkv.shape[0] // 2, width // 4), jnp.bfloat16)
    return call(
        input_body,
        [where, dkv, dq0, dq1, first, second],
        [out, out],
        flops=4 * dkv.shape[0] * width * (first.shape[2] + second.shape[2]),
        name="input_terms",
    )


def in_pairs(start, end, step, carry):
    pairs = (end - start) // 2
    carry = lax.fori_loop(0, pairs, lambda i, v: step(2, start + 2 * i, v), carry)
    return lax.fori_loop(start + 2 * pairs, end, functools.partial(step, 1), carry)


def attention_body(last, scalar_ref, own_slot_ref, other_slot_ref, *refs):
    token_ref, lowest_ref, cosine_ref, sine_ref, query_ref, grad_ref = refs[:6]
    own_refs, other_refs = refs[6 : 6 + SIDE], refs[6 + SIDE : 6 + 2 * SIDE]
    rest = refs[6 + 2 * SIDE :]
    if last:
        before_key_ref, before_value_ref, *rest = rest
        attended_ref, dquery_ref, *rest = rest
        keep_refs, give_refs, scratch = rest[:SIDE], rest[SIDE : 2 * SIDE], rest[2 * SIDE :]
        probs_ref, tops_ref, key_ref, value_ref, dkey_ref, dvalue_ref = scratch
    else:
        attended_ref, dquery_ref, dkey_ref, dvalue_ref, *scratch = rest
        probs_ref, tops_ref, key_ref, value_ref = scratch
    first_block = scalar_ref[0]
    last_block = scalar_ref[1]
    mask_below = scalar_ref[2]
    core = scalar_ref[3]
    rows = 2 * BLOCK
    token = token_ref[...]
    lowest = lowest_ref[...]
    for far in range(SIDE):
        for near in range(SIDE):
            own, other = own_refs[far][near], other_refs[far][near]
            own_block, other_block = own_slot_ref[far * SIDE + near], other_slot_ref[far * SIDE + near]

            @pl.when(core == 0)
            def _():
                key_ref[own_block] = own
                value_ref[other_block] = other

            @pl.when(core == 1)
            def _():
                key_ref[other_block] = other
                value_ref[own_block] = own

    query = jnp.concatenate([query_ref[:, :HEAD_DIM], query_ref[:, HEAD_DIM:]], axis=0)
    grad = jnp.concatenate([grad_ref[:, :HEAD_DIM], grad_ref[:, HEAD_DIM:]], axis=0)
    query_t = query.T
    grad_t = grad.T

    def clear(b):
        dkey_ref[b] = jnp.zeros(dkey_ref.shape[1:], dkey_ref.dtype)
        dvalue_ref[b] = jnp.zeros(dvalue_ref.shape[1:], dvalue_ref.dtype)

    pl.loop(0, first_block)(clear)
    pl.loop(last_block + 1, PLANE)(clear)

    def forward(hide, count, b, carry):
        top, weight, output = carry
        some = pl.ds(b, count)
        keys = key_ref[some].reshape(count * BLOCK, HEAD_DIM)
        scores = jnp.dot(keys, query_t, preferred_element_type=jnp.float32)
        scores = scores * (SCALE * LOG2E)
        if hide:
            position = lax.broadcasted_iota(jnp.int32, scores.shape, 0)
            allowed = (position <= token - b * BLOCK) & (position >= lowest - b * BLOCK)
            scores = jnp.where(allowed, scores, NEG_LARGE)
        new_top = jnp.maximum(top, jnp.max(scores, axis=0, keepdims=True))
        probs = jnp.exp2(scores - new_top)
        fade = jnp.exp2(top - new_top)
        rounded = probs.astype(jnp.bfloat16)
        probs_ref[some] = rounded.reshape(count, BLOCK, rows)
        tops_ref[some] = jnp.broadcast_to(new_top[None], (count, 1, rows))
        weight = weight * fade + jnp.sum(probs, axis=0, keepdims=True)
        values_t = value_ref[some].reshape(count * BLOCK, HEAD_DIM).T
        output = output * fade + jnp.dot(values_t, rounded, preferred_element_type=jnp.float32)
        return new_top, weight, output

    carry = (
        jnp.full((1, rows), NEG_LARGE, jnp.float32),
        jnp.zeros((1, rows), jnp.float32),
        jnp.zeros((HEAD_DIM, rows), jnp.float32),
    )
    hidden_end = jnp.minimum(mask_below + 1, last_block)
    carry = lax.fori_loop(first_block, hidden_end, functools.partial(forward, True, 1), carry)
    carry = in_pairs(hidden_end, last_block, functools.partial(forward, False), carry)
    top, weight, output = forward(True, 1, last_block, carry)
    inverse = 1.0 / weight
    attended_t = output * inverse
    attended = attended_t.T.astype(jnp.bfloat16)
    attended_ref[:, :HEAD_DIM] = attended[:BLOCK]
    attended_ref[:, HEAD_DIM:] = attended[BLOCK:]
    delta = jnp.sum(
        attended_t.astype(jnp.bfloat16).astype(jnp.float32) * grad_t.astype(jnp.float32),
        axis=0,
        keepdims=True,
    )

    def backward(count, b, dquery):
        some = pl.ds(b, count)
        keys = key_ref[some].reshape(count * BLOCK, HEAD_DIM)
        values = value_ref[some].reshape(count * BLOCK, HEAD_DIM)
        prob_grad = jnp.dot(values, grad_t, preferred_element_type=jnp.float32)
        fades = jnp.exp2(tops_ref[some] - top) * inverse
        probs = probs_ref[some].astype(jnp.float32) * fades
        probs = probs.reshape(count * BLOCK, rows)
        score_grad = (probs * (prob_grad - delta)).astype(jnp.bfloat16)
        area = (count, BLOCK, HEAD_DIM)
        dvalue_ref[some] = jnp.dot(
            probs.astype(jnp.bfloat16), grad, preferred_element_type=jnp.float32
        ).reshape(area).astype(dvalue_ref.dtype)
        dkey_ref[some] = jnp.dot(
            score_grad, query, preferred_element_type=jnp.float32
        ).reshape(area).astype(dkey_ref.dtype)
        return dquery + jnp.dot(keys.T, score_grad, preferred_element_type=jnp.float32)

    dquery = in_pairs(
        first_block, last_block + 1, backward, jnp.zeros((HEAD_DIM, rows), jnp.float32)
    )
    dquery = dquery.T * SCALE
    cosine, sine = cosine_ref[...], sine_ref[...]
    for h in range(2):
        dquery_ref[:, h * HEAD_DIM : (h + 1) * HEAD_DIM] = turn(
            dquery[h * BLOCK : (h + 1) * BLOCK], cosine, sine, -1.0
        ).astype(jnp.bfloat16)

    if last:
        for far in range(SIDE):
            for near in range(SIDE):
                slot = far * SIDE + near
                own_block, other_block = own_slot_ref[slot], other_slot_ref[slot]

                @pl.when(core == 0)
                def _():
                    keep_refs[far][near] = (dkey_ref[own_block] + before_key_ref[own_block]).astype(
                        jnp.bfloat16
                    )
                    give_refs[far][near] = (
                        dvalue_ref[other_block] + before_value_ref[other_block]
                    ).astype(jnp.bfloat16)

                @pl.when(core == 1)
                def _():
                    keep_refs[far][near] = (
                        dvalue_ref[own_block] + before_value_ref[own_block]
                    ).astype(jnp.bfloat16)
                    give_refs[far][near] = (dkey_ref[other_block] + before_key_ref[other_block]).astype(
                        jnp.bfloat16
                    )


def attention(scalars, own_slots, other_slots, *inputs, before=()):
    rows = 2 * BLOCK
    query = inputs[4]
    wide = jax.ShapeDtypeStruct(query.shape, jnp.bfloat16)
    area = (PLANE, BLOCK, HEAD_DIM)
    scratch = [
        pltpu.VMEM((PLANE, BLOCK, rows), jnp.bfloat16),
        pltpu.VMEM((PLANE, 1, rows), jnp.float32),
        pltpu.VMEM(area, jnp.bfloat16),
        pltpu.VMEM(area, jnp.bfloat16),
    ]
    if before:
        sums = [jax.ShapeDtypeStruct((SIDE, BLOCK, HEAD_DIM), jnp.bfloat16)] * (2 * SIDE)
        scratch += [pltpu.VMEM(area, jnp.float32)] * 2
    else:
        sums = [jax.ShapeDtypeStruct(area, jnp.bfloat16)] * 2
    return call(
        functools.partial(attention_body, bool(before)),
        [scalars, own_slots, other_slots, *inputs, *before],
        [wide, wide, *sums],
        scalars=3,
        limit=36,
        flops=PLANE * BLOCK * rows * HEAD_DIM * 12,
        scratch=scratch,
        name="attention",
    )


def shards(hidden, w_query, w_key, w_value, out_grad, lengths, advantages):
    x, y = lax.axis_index("x"), lax.axis_index("y")
    zl, zh, c = lax.axis_index("zl"), lax.axis_index("zh"), lax.axis_index("c")
    where = jnp.stack([x, y, zl, c]).astype(jnp.int32)
    local_tokens, width = hidden.shape
    half_cols = w_query.shape[1] // 2

    w_half0 = jnp.concatenate([w_key, w_query[:, :half_cols]], axis=1)
    w_half1 = jnp.concatenate([w_value, w_query[:, half_cols:]], axis=1)
    w_own, w_other = regroup(w_half0, w_half1, zl, c)
    rows_by_half = in_order(w_own, w_other, zl)

    rows = jnp.concatenate(rows_by_half, axis=0)
    pieces = [rows] + [cross_push(rows, SIDE - s, True) for s in (1, 2, 3)]

    z_pairs = []
    for a in range(2):
        for b in range(2):
            for d in range(2):
                z_pairs.append((a * 4 + b * 2 + d, (1 - a) * 4 + (b ^ d) * 2 + d))
    hidden_later, _ = after(hidden, pieces[1:])
    hidden_other = lax.ppermute(hidden_later, ("zl", "zh", "c"), z_pairs)
    hidden_t = call(
        transpose_body,
        [where, hidden, hidden_other],
        [jax.ShapeDtypeStruct((width, 2 * local_tokens), jnp.bfloat16)],
        name="transpose",
    )[0]
    out_grad, _ = after(out_grad, hidden_other)

    first_cols = 3 * HEAD_DIM
    first_line = jnp.concatenate([p[:, :first_cols] for p in pieces], axis=0)
    second_line = jnp.concatenate([p[:, first_cols:] for p in pieces], axis=0)
    first_strips = [first_line] + [cross_push(first_line, SIDE - s, False) for s in (1, 2, 3)]

    block = x * SIDE + y
    tokens = block * BLOCK + jnp.arange(BLOCK, dtype=jnp.int32)
    boundary = jnp.cumsum(lengths)
    segment = jnp.sum((tokens[:, None] >= boundary[None, :]).astype(jnp.int32), axis=1)
    member = segment[:, None] == jnp.arange(lengths.shape[0], dtype=jnp.int32)[None, :]
    start = jnp.sum(jnp.where(member, (boundary - lengths)[None, :], 0), axis=1)
    exponent = jnp.arange(HALF, dtype=jnp.float32) * (2.0 / HEAD_DIM)
    inverse = jnp.exp(-math.log(ROPE_THETA) * exponent)
    angles = (tokens - start).astype(jnp.float32)[:, None] * inverse[None, :]
    cosine, sine = jnp.cos(angles), jnp.sin(angles)
    cosine = jnp.concatenate([cosine, cosine], axis=1)
    sine = jnp.concatenate([-sine, sine], axis=1)
    kv_cosine = jnp.where(c == 0, cosine, 1.0)
    kv_sine = jnp.where(c == 0, sine, 0.0)
    cosines, sines = jnp.stack([kv_cosine, cosine]), jnp.stack([kv_sine, sine])

    own_tokens = block * BLOCK + zl * local_tokens + jnp.arange(local_tokens, dtype=jnp.int32)
    own_segment = jnp.sum((own_tokens[:, None] >= boundary[None, :]).astype(jnp.int32), axis=1)
    own_member = own_segment[:, None] == jnp.arange(lengths.shape[0], dtype=jnp.int32)[None, :]
    own_advantage = jnp.sum(jnp.where(own_member, advantages[None, :], 0.0), axis=1)
    token_grad = (out_grad.astype(jnp.float32) * own_advantage[:, None]).astype(jnp.bfloat16)
    tg_own, tg_other = regroup(token_grad[:, :half_cols], token_grad[:, half_cols:], zl, c)
    grad = jnp.concatenate(in_order(tg_own, tg_other, zl), axis=0)

    kv, query0, w_first = project(
        ((0, 1), (1, 2)), where, first_strips, hidden, hidden_other, cosines, sines
    )
    line = jnp.stack([kv] + [cross_push(kv, SIDE - s, True) for s in (1, 2, 3)])
    line, _ = after(line, hidden_t)
    own_lines = [line] + [cross_push(line, SIDE - s, False) for s in (1, 2, 3)]
    other_lines = [swap_core(v) for v in own_lines]
    second_line, _ = after(second_line, own_lines[1:])
    second_strips = [second_line] + [cross_push(second_line, SIDE - s, False) for s in (1, 2, 3)]

    slots = jnp.arange(PLANE, dtype=jnp.int32)
    far, near = slots // SIDE, slots % SIDE
    x_near = ((x + near) % SIDE) * SIDE + (y + far) % SIDE
    y_near = ((x + far) % SIDE) * SIDE + (y + near) % SIDE
    own_slots = jnp.where(c == 0, x_near, y_near)
    other_slots = jnp.where(c == 0, y_near, x_near)
    scalars = jnp.stack([start[0] // BLOCK, block, start[BLOCK - 1] // BLOCK, c]).astype(jnp.int32)
    token_row = jnp.concatenate([tokens, tokens])[None, :]
    lowest_row = jnp.concatenate([start, start])[None, :]
    pair_cols = 2 * HEAD_DIM

    def attend(query, pair_grad, before=()):
        tables = (token_row, lowest_row, cosine, sine)
        lines = (*own_lines, *other_lines)
        return attention(
            scalars, own_slots, other_slots, *tables, query, pair_grad, *lines, before=before
        )

    attended0, dquery0, *before = attend(query0, grad[:, :pair_cols])
    terms0 = weight_terms(where, hidden_t, dquery0)
    moved0 = [cross_push(terms0[s], s, False) for s in (1, 2, 3)]

    query1, w_second = project(((1, 2),), where, second_strips, hidden, hidden_other, cosines, sines)
    query1, _ = after(query1, terms0[0])
    attended1, dquery1, *sums = attend(query1, grad[:, pair_cols:], before)
    keep, give = sums[:SIDE], after(sums[SIDE:], moved0)[0]
    area = [total([keep[s], swap_core(give[s])]) for s in (1, 2, 3, 0)]
    area = [area[3], *area[:3]]
    line = total([area[0]] + [cross_push(area[s], s, False) for s in (1, 2, 3)])
    dkv = line[0].astype(jnp.float32)
    for s in (1, 2, 3):
        dkv = dkv + cross_push(line[s], s, True).astype(jnp.float32)
    dkv = dkv * jnp.where(c == 0, SCALE, 1.0)
    swapped = jnp.concatenate([dkv[:, HALF:], dkv[:, :HALF]], axis=1)
    dkv = (dkv * kv_cosine - swapped * kv_sine).astype(jnp.bfloat16)

    sum0 = total([terms0[0]] + moved0)
    terms1, _ = after(weight_terms(where, hidden_t, dquery1), area)
    moved1 = [cross_push(terms1[s], s, False) for s in (1, 2, 3)]
    sum1 = total([terms1[0]] + moved1)
    attended = jnp.concatenate([attended0, attended1], axis=1)
    attended, _ = after(attended, dkv)
    at0, at1 = attended[:local_tokens], attended[local_tokens:]
    halves = ungroup(*in_order(at0, at1, zl), zl, c)
    attended_out = jnp.concatenate(halves, axis=1)
    dkv, _ = after(dkv, (moved1[0], halves))
    kv_terms = weight_terms(where, hidden_t, dkv)
    kv_sum = total([kv_terms[0]] + [cross_push(kv_terms[s], s, False) for s in (1, 2, 3)])
    both = jnp.concatenate([kv_sum, sum0, sum1], axis=1)

    keep, give = input_terms(where, after(dkv, kv_terms[0])[0], dquery0, dquery1, w_first, w_second)
    chip = total([keep, swap_core(give)])
    both, _ = after(both, chip)

    small = both.shape[0] // SIDE
    pieces = [both[s * small : (s + 1) * small] for s in range(SIDE)]
    dw_rows = total([pieces[0]] + [cross_push(pieces[s], s, True) for s in (1, 2, 3)])
    dw_rows = dw_rows[: small // 2], dw_rows[small // 2 :]
    dw0, dw1 = ungroup(*in_order(dw_rows[0], dw_rows[1], zl), zl, c)
    grad_w_key = dw0[:, :HEAD_DIM]
    grad_w_value = dw1[:, :HEAD_DIM]
    grad_w_query = jnp.concatenate([dw0[:, HEAD_DIM:], dw1[:, HEAD_DIM:]], axis=1)

    z = zh * 2 + zl
    ring = [(0, 0), (1, 0), (0, 1), (1, 1)]
    parts = [lax.dynamic_index_in_dim(chip, z, 0, keepdims=False)]
    for s in (1, 2, 3):
        pairs = [
            (ring[i][0] * 2 + ring[i][1], ring[(i + s) % 4][0] * 2 + ring[(i + s) % 4][1])
            for i in range(4)
        ]
        piece = lax.dynamic_index_in_dim(chip, (z + s) % 4, 0, keepdims=False)
        parts.append(lax.ppermute(piece, ("zl", "zh"), pairs))
    grad_hidden = total(parts)

    return attended_out, grad_hidden, grad_w_query, grad_w_key, grad_w_value


def solution(mesh):
    fine = Mesh(mesh.devices.reshape(SIDE, SIDE, 2, 2, 2), ("x", "y", "zl", "zh", "c"))
    dp, mp = ("x", "y", "zl"), ("zh", "c")
    return jax.shard_map(
        shards,
        mesh=fine,
        in_specs=(P(dp, None), P(dp, mp), P(dp, mp), P(dp, mp), P(dp, mp), P(), P()),
        out_specs=(P(dp, mp),) * 5,
        check_vma=False,
    )
```
